256 devices in a mesh: gx: 8 (over z_lo, y), gy: 16 (over x, z_hi), row: 2 (over core).
Axes of the slice: x: 4, y: 4, z: 8 (z_hi: 4, z_lo: 2; z = z_hi * 2 + z_lo), core: 2. Of those that a mesh axis runs over, the one named last changes fastest.
Arguments:
- initial_velocity: float32 [16, 512, 4096], P('row', 'gx', 'gy'), may hold values from -6 to 6
- background_speed: float32 [512, 4096], P('gx', 'gy'), may hold values from 0.98 to 1
- density: float32 [512, 4096], P('gx', 'gy'), may hold values from 1.5 to 3
- east_modes: float32 [512, 96], P('gx', 'gy'), may hold values from -0.625 to 0.625
- north_modes: float32 [96, 4096], P('gx', 'gy'), may hold values from -0.625 to 0.625
- mode_coef: float32 [16, 96, 96], P('row', 'gy'), may hold values from -5 to 5
Outputs:
- peak_velocity: float32 [16, 512, 4096], P('row', 'gx', 'gy')
The draws below stay inside these ranges and needn't reach their ends.
All inputs are finite; a program needn't handle non-finite values.
Results may differ from the reference program's by a relative error of at most 0.00011.
Values sent between devices are 32-bit elements; how exact they have to be, the bound alone decides.
A program may use at most 64 MiB of HBM per device.

```python
import jax
import jax.numpy as jnp
from jax import lax

K = 96
CX = 64
CY = 256
STEPS = 6
NX = 512
NY = 4096
R = 16


def band_rows(total, tile):
    place = jnp.arange(total) % tile
    depth = jnp.minimum(place, tile - 1 - place)
    return (depth >= 5) & (depth <= 17)


def draw_initial_velocity(key, part):
    key = jax.random.fold_in(key, 2)
    key_inner, key_size = jax.random.split(key)
    inner = jnp.clip(jax.random.normal(key_inner, (R, NX, NY), jnp.float32), -6.0, 6.0)
    size = jax.random.uniform(key_size, (R, NX, NY), jnp.float32, 3.0, 6.0)
    band = band_rows(NX, CX)[:, None] | band_rows(NY, CY)[None, :]
    parity = (jnp.arange(NX)[:, None] + jnp.arange(NY)[None, :]) % 2
    checker = 1.0 - 2.0 * parity.astype(jnp.float32)
    return jnp.where(band[None], checker[None] * size, inner).astype(jnp.float32)


def draw_background_speed(key, part):
    key = jax.random.fold_in(key, 1)
    unit = jax.random.uniform(key, (NX, NY), jnp.float32, 0.0, 1.0)
    values = 0.98 + 0.02 * unit
    return values.astype(jnp.float32)


def block_scale(own_key, extent, shards, least, high):
    loudness = 1.0
    for axis_at, blocks in shards:
        draws = jax.random.uniform(jax.random.fold_in(jax.random.fold_in(own_key, 6), axis_at), (blocks,), jnp.float32, least / len(shards), high / len(shards))
        loudness = loudness * jnp.repeat(jnp.exp(draws), extent[axis_at] // blocks).reshape((-1,) + (1,) * (len(extent) - 1 - axis_at))
    return loudness


def bell_draw(own_key, extent, spread, most, shards=(), dtype=jnp.bfloat16):
    gain = block_scale(own_key, extent, shards, -0.22, 0.18) if shards else 1.0
    result = jax.random.normal(own_key, extent, jnp.float32) * spread * gain
    return jnp.minimum(jnp.maximum(result, -most), most).astype(dtype)


def setup_inputs(seed: int = 0) -> dict:
    key_of = jax.random.split(jax.random.key(seed), 7)
    return {
        "initial_velocity": draw_initial_velocity(jax.random.fold_in(key_of[6], 71), 0),
        "background_speed": draw_background_speed(jax.random.fold_in(key_of[6], 71), 0),
        "density": jnp.clip(1.5 + 1.5 * jax.random.uniform(key_of[2], (NX, NY), jnp.float32) ** block_scale(key_of[2], (NX, NY), ((0, 8), (1, 16)), -0.2, 0.2), 1.5, 3.0),
        "east_modes": bell_draw(key_of[3], (NX, K), K ** -0.5, 0.625, ((0, 8), (1, 16)), jnp.float32),
        "north_modes": bell_draw(key_of[4], (K, NY), K ** -0.5, 0.625, ((0, 8), (1, 16)), jnp.float32),
        "mode_coef": bell_draw(key_of[5], (R, K, K), 1.0, 5.0, ((0, 2), (1, 16)), jnp.float32),
    }


coef_near = 9.0 / 8.0
coef_far = -1.0 / 24.0
time_step = 0.55
perturb_gain = 0.03


def one_realization(start_field, coef_block, background_speed, density, east_modes, north_modes):
    panel = jnp.dot(east_modes, coef_block, precision=lax.Precision.HIGHEST, preferred_element_type=jnp.float32)
    shape_field = jnp.dot(panel, north_modes, precision=lax.Precision.HIGHEST, preferred_element_type=jnp.float32)
    speed = background_speed * (1.0 + perturb_gain * jnp.tanh(shape_field))
    modulus = density * speed * speed
    size_x, size_y = start_field.shape
    velocity = start_field
    stress_east = jnp.zeros_like(start_field)
    stress_north = jnp.zeros_like(start_field)
    peak = jnp.zeros_like(start_field)
    for step in range(STEPS):
        padded = jnp.pad(velocity, ((2, 2), (2, 2)))
        mid = padded[:, 2:size_y + 2]
        grad_east = coef_near * (mid[3:size_x + 3] - mid[2:size_x + 2]) + coef_far * (mid[4:size_x + 4] - mid[1:size_x + 1])
        mid = padded[2:size_x + 2, :]
        grad_north = coef_near * (mid[:, 3:size_y + 3] - mid[:, 2:size_y + 2]) + coef_far * (mid[:, 4:size_y + 4] - mid[:, 1:size_y + 1])
        stress_east = stress_east + time_step * modulus * grad_east
        stress_north = stress_north + time_step * modulus * grad_north
        east_pad = jnp.pad(stress_east, ((2, 2), (0, 0)))
        north_pad = jnp.pad(stress_north, ((0, 0), (2, 2)))
        div_east = coef_near * (east_pad[2:size_x + 2] - east_pad[1:size_x + 1]) + coef_far * (east_pad[3:size_x + 3] - east_pad[0:size_x])
        div_north = coef_near * (north_pad[:, 2:size_y + 2] - north_pad[:, 1:size_y + 1]) + coef_far * (north_pad[:, 3:size_y + 3] - north_pad[:, 0:size_y])
        velocity = velocity + time_step / density * (div_east + div_north)
        peak = jnp.maximum(peak, jnp.abs(velocity))
    return peak


def reference(initial_velocity, background_speed, density, east_modes, north_modes, mode_coef):
    def apply_one(pair):
        return one_realization(pair[0], pair[1], background_speed, density, east_modes, north_modes)

    return lax.map(apply_one, (initial_velocity, mode_coef))
```

```python
import functools

import jax
import jax.numpy as jnp
from jax import lax
from jax.experimental import pallas as pl
from jax.experimental.pallas import tpu as pltpu
from jax.sharding import PartitionSpec as P

MESH = pl.DeviceIdType.MESH
F32 = jnp.float32
STEPS = 6
HALO = 3 * STEPS
OFF = 24
LANES = 128
SUB = 8
PER = LANES // HALO
UNROLL = 4
SCALE = 0.55 / 24.0
GAIN = 0.03


def roll(x, shift, axis=1):
    shift %= x.shape[axis]
    return pltpu.roll(x, shift, axis) if shift else x


def lane_index():
    return lax.broadcasted_iota(jnp.int32, (SUB, LANES), 1)


def widen(lane, west, t0, t1, east):
    return (
        jnp.where(lane < HALO, west, roll(t0, HALO)),
        jnp.where(lane < 64, roll(t0, 64), roll(t1, 64)),
        jnp.where(lane < LANES - HALO, roll(t1, -HALO), east),
    )


E_LO, E_HI, N_LO, N_HI, V_LO, V_HI, DB_LO, DB_HI, S_LO, S_HI, LL, LH, HL, HH = range(14)


def kernel(
    dims,
    v_hbm,
    bg_hbm,
    d_hbm,
    e_hbm,
    n_hbm,
    c_hbm,
    out_ref,
    v_in,
    db_in,
    e_in,
    n_in,
    c_in,
    pad_c,
    pad_e,
    pad_n,
    cg,
    eg,
    ng,
    e_own,
    e_halo,
    n_edge,
    n_halo,
    vt,
    v_halo,
    db_halo,
    strip,
    strip_halo,
    corner_lo,
    corner_hi,
    panel,
    dens,
    speed,
    vel,
    mod,
    buoy,
    s_e,
    s_n,
    peak,
    flat,
    load_sem,
    send_sem,
    recv_sem,
):
    gx_n, gy_n, y_n, kx, ky = dims
    x_n = gy_n // y_n
    gx, gy = lax.axis_index("gx"), lax.axis_index("gy")
    outer, inner = gy // y_n, lax.rem(gy, y_n)
    lane = lane_index()
    sub = lax.broadcasted_iota(jnp.int32, (SUB, LANES), 0)

    def gxo(o):
        return lax.rem(gx + o + gx_n, gx_n)

    def gyo(o):
        return lax.rem(gy + o + gy_n, gy_n)

    def peer(e, d):
        return lax.rem(outer + e, x_n) * y_n + lax.rem(inner + d, y_n)

    loads = [
        pltpu.make_async_copy(src, dst, load_sem.at[i])
        for i, (src, dst) in enumerate(
            (
                (e_hbm, e_in),
                (n_hbm, n_in),
                (c_hbm, c_in),
                (v_hbm, v_in),
                (d_hbm, db_in.at[0]),
                (bg_hbm, db_in.at[1]),
            )
        )
    ]
    for load in loads:
        load.start()

    partners = [{"gx": gxo(a), "gy": gyo(b)} for a in (-1, 0, 1) for b in (-1, 0, 1) if a or b]
    partners += [{"gy": peer(0, d)} for d in range(1, y_n)]
    partners += [{"gy": peer(e, 0)} for e in range(1, x_n)]
    partners += [{"gx": gxo(o)} for o in range(1, gx_n)]
    barrier = pltpu.get_barrier_semaphore()
    for partner in partners:
        pl.semaphore_signal(barrier, inc=1, device_id=partner, device_id_type=MESH)

    sent = []

    def send(src, dst, slot, target):
        copy = pltpu.make_async_remote_copy(
            src_ref=src,
            dst_ref=dst,
            send_sem=send_sem.at[len(sent)],
            recv_sem=recv_sem.at[slot],
            device_id=target,
            device_id_type=MESH,
        )
        copy.start()
        sent.append(copy)

    def arrived(dst, slot):
        pltpu.make_async_copy(dst, dst, recv_sem.at[slot]).wait()

    c_base = 14
    e_base = c_base + gy_n
    n_base = e_base + gy_n

    pad_c[...] = jnp.zeros_like(pad_c)
    pad_e[...] = jnp.zeros_like(pad_e)
    pad_n[...] = jnp.zeros_like(pad_n)
    for load in loads[:3]:
        load.wait()
    pad_e[0 : e_in.shape[0], 0:ky] = e_in[...]
    pad_n[0:kx, :] = n_in[...]
    pad_c[:, 0:ky, 0 : c_in.shape[2]] = c_in[...]

    e_own[...] = roll(jnp.transpose(pad_e[...])[0:SUB], OFF)
    n0, n1 = (pad_n[0:SUB, 0:LANES], pad_n[0:SUB, LANES:]), (pad_n[SUB:, 0:LANES], pad_n[SUB:, LANES:])
    n_edge[0] = jnp.where(lane < HALO, n0[0], roll(n1[0], HALO))
    n_edge[1] = jnp.where(lane < HALO, roll(n0[1], HALO), roll(n1[1], 2 * HALO))

    spread = []
    for r in range(SUB):
        whole = pad_c[r]
        wide = jnp.zeros_like(whole)
        for block in range(gx_n):
            keep = (lane >= 16 * block) & (lane < 16 * block + kx)
            wide = jnp.where(keep, roll(whole, (16 - kx) * block), wide)
        spread.append(wide)
    for r in range(6):
        extra = spread[6 + r // 3]
        cg[0, r] = jnp.where(sub < ky, spread[r], roll(extra, ky - 2 * (r % 3), 0))

    pl.semaphore_wait(barrier, len(partners))

    send(e_own, e_halo.at[0], E_LO, {"gx": gxo(1)})
    send(e_own, e_halo.at[1], E_HI, {"gx": gxo(-1)})
    send(n_edge.at[1], n_halo.at[0], N_LO, {"gy": gyo(1)})
    send(n_edge.at[0], n_halo.at[1], N_HI, {"gy": gyo(-1)})
    for d in range(1, y_n):
        send(cg.at[0], cg.at[d], c_base + d, {"gy": peer(0, d)})
    for e in range(1, x_n):
        send(cg.at[0], cg.at[e * y_n], c_base + e * y_n, {"gy": peer(e, 0)})

    loads[4].wait()
    loads[5].wait()
    rows = db_in.shape[1]
    send(db_in.at[:, pl.ds(rows - OFF, OFF)], db_halo.at[0], DB_LO, {"gx": gxo(1)})
    send(db_in.at[:, pl.ds(0, OFF)], db_halo.at[1], DB_HI, {"gx": gxo(-1)})

    loads[3].wait()

    @pl.loop(0, rows // SUB)
    def _(a):
        at = pl.multiple_of(a * SUB, SUB)
        for r in range(SUB):
            for t in range(2):
                vt[t, pl.ds(a * SUB * SUB + r, SUB, stride=SUB), :] = v_in[
                    r, pl.ds(at, SUB), t * LANES : (t + 1) * LANES
                ]

    edge = HALO * SUB
    send(vt.at[:, pl.ds(rows * SUB - edge, edge)], v_halo.at[0], V_LO, {"gx": gxo(1)})
    send(vt.at[:, pl.ds(0, edge)], v_halo.at[1], V_HI, {"gx": gxo(-1)})

    def tile(t, i):
        return vt[t, pl.ds(pl.multiple_of(i * SUB, SUB), SUB), :]

    full = rows // PER

    def pack(g, count):
        low = jnp.zeros((SUB, LANES), F32)
        high = jnp.zeros((SUB, LANES), F32)
        for p in range(count):
            here = (lane >= p * HALO) & (lane < (p + 1) * HALO)
            low = jnp.where(here, roll(tile(0, g * PER + p), p * HALO), low)
            high = jnp.where(here, roll(tile(1, g * PER + p), (p + 1) * HALO), high)
        strip[0, 1 + g] = low
        strip[1, 1 + g] = high

    pl.loop(0, full)(lambda g: pack(g, PER))
    slabs = full
    if rows % PER:
        pack(full, rows % PER)
        slabs += 1
    lo_tile, hi_tile = 0, rows // SUB - 3
    groups = ((0, range(0, 3)), (slabs + 1, range(hi_tile, hi_tile + 3)), (slabs + 2, range(3, hi_tile)))
    for slab, blocks in groups:
        low = jnp.zeros((SUB, LANES), F32)
        high = jnp.zeros((SUB, LANES), F32)
        for j, a in enumerate(blocks):
            for q in range(2):
                p = 2 * j + q
                here = (lane >= p * HALO) & (lane < (p + 1) * HALO)
                low = jnp.where(here, roll(db_in[q, a * SUB : (a + 1) * SUB, 0:LANES], p * HALO), low)
                high = jnp.where(here, roll(db_in[q, a * SUB : (a + 1) * SUB, LANES:], (p + 1) * HALO), high)
        strip[0, slab] = low
        strip[1, slab] = high
    first_hi = (rows - HALO) // PER
    lo_len, hi_len = corner_hi.shape[1], corner_lo.shape[1]
    lo_rows, hi_rows = pl.ds(0, lo_len), pl.ds(1 + first_hi, hi_len)
    send(strip.at[1], strip_halo.at[0], S_LO, {"gy": gyo(1)})
    send(strip.at[0], strip_halo.at[1], S_HI, {"gy": gyo(-1)})
    send(strip.at[1, hi_rows], corner_lo.at[0], LL, {"gx": gxo(1), "gy": gyo(1)})
    send(strip.at[0, hi_rows], corner_lo.at[1], LH, {"gx": gxo(1), "gy": gyo(-1)})
    send(strip.at[1, lo_rows], corner_hi.at[0], HL, {"gx": gxo(-1), "gy": gyo(1)})
    send(strip.at[0, lo_rows], corner_hi.at[1], HH, {"gx": gxo(-1), "gy": gyo(-1)})

    arrived(e_halo.at[0], E_LO)
    arrived(e_halo.at[1], E_HI)
    eg[0] = jnp.where(
        lane < OFF, roll(e_halo[0], -rows), jnp.where(lane < OFF + rows, e_own[...], roll(e_halo[1], rows))
    )
    for d in range(1, y_n):
        send(eg.at[0], eg.at[d], e_base + d, {"gy": peer(0, d)})
    for e in range(1, x_n):
        send(eg.at[0], eg.at[e * y_n], e_base + e * y_n, {"gy": peer(e, 0)})
    arrived(n_halo.at[0], N_LO)
    arrived(n_halo.at[1], N_HI)
    for half, (t0, t1) in enumerate((n0, n1)):
        west = roll(n_halo[0], -half * HALO)
        east = roll(n_halo[1], -(half + 1) * HALO)
        for t, value in enumerate(widen(lane, west, t0, t1, east)):
            ng[gx, t, half * SUB : (half + 1) * SUB, :] = value
    for o in range(1, gx_n):
        send(ng.at[gx], ng.at[gx], n_base + o, {"gx": gxo(o)})

    for d in sorted(range(1, y_n), key=lambda d: min(d, y_n - d)):
        arrived(cg.at[d], c_base + d)
        for e in range(1, x_n):
            send(cg.at[d], cg.at[e * y_n + d], c_base + e * y_n + d, {"gy": peer(e, 0)})
    for d in sorted(range(1, y_n), key=lambda d: min(d, y_n - d)):
        arrived(eg.at[d], e_base + d)
        for e in range(1, x_n):
            send(eg.at[d], eg.at[e * y_n + d], e_base + e * y_n + d, {"gy": peer(e, 0)})

    west_in, east_in = gy > 0, gy < gy_n - 1
    low_in, high_in = gx > 0, gx < gx_n - 1
    one = jnp.float32(1.0)
    west_gain, east_gain = jnp.where(west_in, one, 0.0), jnp.where(east_in, one, 0.0)
    low_gain, high_gain = jnp.where(low_in, one, 0.0), jnp.where(high_in, one, 0.0)

    arrived(strip_halo.at[0], S_LO)
    arrived(strip_halo.at[1], S_HI)

    def own_rows(g, count):
        for p in range(count):
            i = g * PER + p
            west = roll(strip_halo[0, 1 + g], -p * HALO) * west_gain
            east = roll(strip_halo[1, 1 + g], -(p + 1) * HALO) * east_gain
            for t, value in enumerate(widen(lane, west, tile(0, i), tile(1, i), east)):
                vel[t, OFF + i] = value

    pl.loop(0, full)(lambda g: own_rows(g, PER))
    if rows % PER:
        own_rows(full, rows % PER)

    for side, slot in ((0, V_LO), (1, V_HI)):
        arrived(v_halo.at[side], slot)
    for side, slot in ((0, LL), (1, LH)):
        arrived(corner_lo.at[side], slot)
    for side, slot in ((0, HL), (1, HH)):
        arrived(corner_hi.at[side], slot)
    zero = jnp.zeros((SUB, LANES), F32)
    for t in range(3):
        for i in range(OFF - HALO):
            vel[t, i] = zero
            vel[t, OFF + rows + HALO + i] = zero
    for i in range(HALO):
        for side, corner, row, at, gain in (
            (0, corner_lo, rows - HALO + i, OFF - HALO + i, low_gain),
            (1, corner_hi, i, OFF + rows + i, high_gain),
        ):
            slab = row // PER - first_hi if side == 0 else 1 + row // PER
            p = row % PER
            west = roll(corner[0, slab], -p * HALO) * west_gain
            east = roll(corner[1, slab], -(p + 1) * HALO) * east_gain
            t0 = v_halo[side, 0, i * SUB : (i + 1) * SUB, :]
            t1 = v_halo[side, 1, i * SUB : (i + 1) * SUB, :]
            for t, value in enumerate(widen(lane, west, t0, t1, east)):
                vel[t, at] = value * gain

    for side, slot in ((0, DB_LO), (1, DB_HI)):
        arrived(db_halo.at[side], slot)
    tiles = rows // SUB
    for b in range(tiles + 6):
        values = []
        for q in range(2):
            if b < 3:
                t0, t1 = (db_halo[0, q, b * SUB : (b + 1) * SUB, t * LANES : (t + 1) * LANES] for t in range(2))
                w, e = (corner_lo[s, hi_len - 1] for s in range(2))
                p = 2 * b + q
            elif b < tiles + 3:
                a = b - 3
                t0, t1 = (db_in[q, a * SUB : (a + 1) * SUB, t * LANES : (t + 1) * LANES] for t in range(2))
                slab, blocks = next(g for g in groups if a in g[1])
                w, e = (strip_halo[s, slab] for s in range(2))
                p = 2 * (a - blocks[0]) + q
            else:
                a = b - 3 - tiles
                t0, t1 = (db_halo[1, q, a * SUB : (a + 1) * SUB, t * LANES : (t + 1) * LANES] for t in range(2))
                w, e = (corner_hi[s, 0] for s in range(2))
                p = 2 * a + q
            values.append(widen(lane, roll(w, -p * HALO), t0, t1, roll(e, -(p + 1) * HALO)))
        for t in range(3):
            d, s = values[0][t], values[1][t]
            gains = ([low_gain] if b < 3 else []) + ([high_gain] if b >= tiles + 3 else [])
            keep = jnp.ones((SUB, LANES), F32)
            if t == 0:
                keep = jnp.where(lane < HALO, west_gain, keep)
            if t == 2:
                keep = jnp.where(lane >= LANES - HALO, east_gain, keep)
            for gain in gains:
                keep = keep * gain
            speed[t, b * SUB : (b + 1) * SUB, :] = (keep * SCALE) * d * s * s
            dens[t, b * SUB : (b + 1) * SUB, :] = (keep * SCALE) / d

    for slot in range(1, gy_n):
        if slot >= y_n:
            arrived(cg.at[slot], c_base + slot)
            arrived(eg.at[slot], e_base + slot)
    depth = gy_n * SUB
    wide_rows = OFF + rows + OFF
    lhs = jnp.transpose(eg[...].reshape(depth, LANES))[0:wide_rows]
    shifted = []
    for s in range(3):
        parts = [jnp.where(sub >= ky, roll(eg[b], ky - 2 * s, 0), 0.0) for b in range(gy_n)]
        shifted.append(jnp.transpose(jnp.concatenate(parts, axis=0))[0:wide_rows])

    def product(a, b):
        return jnp.dot(a, b, precision=lax.Precision.HIGHEST, preferred_element_type=F32)

    last = [None, None]
    for r in range(6):
        rhs = cg[:, r].reshape(depth, LANES)
        panel[pl.ds(r, wide_rows, stride=SUB), :] = product(lhs, rhs)
        term = product(shifted[r % 3], rhs)
        last[r // 3] = term if last[r // 3] is None else last[r // 3] + term
    for r in (6, 7):
        panel[pl.ds(r, wide_rows, stride=SUB), :] = last[r - 6]

    for o in range(1, gx_n):
        at = gxo(-o)
        arrived(ng.at[at], n_base + o)
    if gx_n * 16 < LANES:
        panel_depth = gx_n * 16
    else:
        panel_depth = LANES
    right = jnp.concatenate([ng[:, t].reshape(gx_n * 16, LANES) for t in range(3)], axis=1)

    @pl.loop(0, wide_rows // SUB)
    def _(c):
        at = pl.multiple_of(c * SUB, SUB)
        left = panel[pl.ds(pl.multiple_of(c * SUB * SUB, SUB * SUB), SUB * SUB), :]
        field = product(left[:, 0:panel_depth], right)
        for t in range(3):
            g = speed[t, pl.ds(at, SUB), :]
            w = dens[t, pl.ds(at, SUB), :]
            for u in range(SUB):
                q = 1.0 + GAIN * jnp.tanh(field[u * SUB : (u + 1) * SUB, t * LANES : (t + 1) * LANES])
                mod[t, at + u] = jnp.broadcast_to(g[u : u + 1], (SUB, LANES)) * (q * q)
                buoy[t, at + u] = jnp.broadcast_to(w[u : u + 1], (SUB, LANES))

    for step in range(1, STEPS + 1):
        begin = OFF - HALO + 3 * step - 2
        count = rows + 2 * HALO + 3 - 6 * step
        chunks = -(-count // UNROLL)

        def sweep(c, carry, begin=begin, first=step == 1):
            carry = list(carry)
            for u in range(UNROLL):
                i = begin + c * UNROLL + u
                for t in range(3):
                    vm, v0, v1, e3, e2, e1, n1_ = carry[t]
                    v2 = vel[t, i + 2]
                    m = mod[t, i]
                    ge = 27.0 * (v1 - v0) - (v2 - vm)
                    gn = 27.0 * (roll(v0, -1) - v0) - (roll(v0, -2) - roll(v0, 1))
                    se, sn = m * ge, m * gn
                    if not first:
                        se, sn = s_e[t, i] + se, s_n[t, i] + sn
                    if step < STEPS:
                        s_e[t, i] = se
                        s_n[t, i] = sn
                    near = (e1 - e2) + (n1_ - roll(n1_, 1))
                    far = (se - e3) + (roll(n1_, -1) - roll(n1_, 2))
                    vn = vm + buoy[t, i - 1] * (27.0 * near - far)
                    if step < STEPS:
                        vel[t, i - 1] = vn
                    top = jnp.abs(vn)
                    peak[t, i - 1] = top if first else jnp.maximum(peak[t, i - 1], top)
                    carry[t] = (v0, v1, v2, e2, e1, se, sn)
            return tuple(carry)

        start = tuple(
            (vel[t, begin - 1], vel[t, begin], vel[t, begin + 1], zero, zero, zero, zero) for t in range(3)
        )
        lax.fori_loop(0, chunks, sweep, start)

    cut_a = LANES - 2 * HALO
    cut_b = 174 - LANES

    @pl.loop(0, rows // SUB)
    def _(a):
        for u in range(SUB):
            i = a * SUB + u
            p0, p1, p2 = (peak[t, OFF + i] for t in range(3))
            mid = roll(p1, 64)
            at = pl.multiple_of(i * SUB, SUB)
            flat[0, pl.ds(at, SUB), :] = jnp.where(lane < cut_a, roll(p0, -HALO), mid)
            flat[1, pl.ds(at, SUB), :] = jnp.where(lane < cut_b, mid, roll(p2, HALO))
        at = pl.multiple_of(a * SUB, SUB)
        for r in range(SUB):
            for t in range(2):
                out_ref[r, pl.ds(at, SUB), t * LANES : (t + 1) * LANES] = flat[
                    t, pl.ds(a * SUB * SUB + r, SUB, stride=SUB), :
                ]

    for copy in sent:
        copy.wait_send()


def on_device(gx_n, gy_n, initial_velocity, background_speed, density, east_modes, north_modes, mode_coef):
    reals, rows, cols = initial_velocity.shape
    kx, ky = north_modes.shape[0], east_modes.shape[1]
    y_n = 4 if gy_n == 16 else 2
    x_n = gy_n // y_n
    wide = rows + 2 * OFF
    slabs = -(-rows // PER)
    lo_len = 1 + (HALO - 1) // PER + 1
    hi_len = slabs - (rows - HALO) // PER + 1
    sends = 4 + 2 + 2 + 2 + 4 + 2 * (gy_n - 1) + gx_n - 1
    vmem = lambda *shape: pltpu.VMEM(shape, F32)
    scratch = [
        vmem(reals, rows, cols),
        vmem(2, rows, cols),
        vmem(*east_modes.shape),
        vmem(*north_modes.shape),
        vmem(*mode_coef.shape),
        vmem(reals, SUB, LANES),
        vmem(LANES, LANES),
        vmem(16, cols),
        vmem(gy_n, 6, SUB, LANES),
        vmem(gy_n, SUB, LANES),
        vmem(gx_n, 3, 16, LANES),
        vmem(SUB, LANES),
        vmem(2, SUB, LANES),
        vmem(2, SUB, LANES),
        vmem(2, SUB, LANES),
        vmem(2, rows * SUB, LANES),
        vmem(2, 2, HALO * SUB, LANES),
        vmem(2, 2, OFF, cols),
        vmem(2, slabs + 3, SUB, LANES),
        vmem(2, slabs + 3, SUB, LANES),
        vmem(2, hi_len, SUB, LANES),
        vmem(2, lo_len, SUB, LANES),
        vmem(wide * SUB, LANES),
        vmem(3, wide, LANES),
        vmem(3, wide, LANES),
        vmem(3, wide, SUB, LANES),
        vmem(3, wide, SUB, LANES),
        vmem(3, wide, SUB, LANES),
        vmem(3, wide, SUB, LANES),
        vmem(3, wide, SUB, LANES),
        vmem(3, wide, SUB, LANES),
        vmem(2, rows * SUB, LANES),
        pltpu.SemaphoreType.DMA((6,)),
        pltpu.SemaphoreType.DMA((sends,)),
        pltpu.SemaphoreType.DMA((14 + 2 * gy_n + gx_n,)),
    ]
    return pl.pallas_call(
        functools.partial(kernel, (gx_n, gy_n, y_n, kx, ky)),
        out_shape=jax.ShapeDtypeStruct(initial_velocity.shape, F32),
        in_specs=[pl.BlockSpec(memory_space=pl.ANY)] * 6,
        out_specs=pl.BlockSpec(memory_space=pltpu.VMEM),
        scratch_shapes=scratch,
        compiler_params=pltpu.CompilerParams(
            collective_id=0, has_side_effects=True, vmem_limit_bytes=40 * 1024 * 1024
        ),
    )(initial_velocity, background_speed, density, east_modes, north_modes, mode_coef)


def solution(mesh):
    in_specs = (
        P("row", "gx", "gy"),
        P("gx", "gy"),
        P("gx", "gy"),
        P("gx", "gy"),
        P("gx", "gy"),
        P("row", "gy", None),
    )
    out_specs = P("row", "gx", "gy")
    body = functools.partial(on_device, mesh.shape["gx"], mesh.shape["gy"])
    return jax.shard_map(body, mesh=mesh, in_specs=in_specs, out_specs=out_specs, check_vma=False)
```

```python
import functools

import jax
import jax.numpy as jnp
from jax import lax
from jax.experimental import pallas as pl
from jax.experimental.pallas import tpu as pltpu
from jax.sharding import PartitionSpec as P

MESH = pl.DeviceIdType.MESH
F32 = jnp.float32
STEPS = 6
HALO = 3 * STEPS
OFF = 24
LANES = 128
SUB = 8
PER = LANES // HALO
PLANES = 5
HALF = LANES // 2
WIDE = PLANES * LANES
UNROLL = 4
BF16 = jnp.bfloat16
SCALE = 0.55 / 24.0
GAIN = 0.03


def roll(x, shift, axis=1):
    shift %= x.shape[axis]
    return pltpu.roll(x, shift, axis) if shift else x


def lane_index():
    return lax.broadcasted_iota(jnp.int32, (SUB, LANES), 1)


def pieces(x):
    high = x.astype(BF16)
    rest = x - high.astype(F32)
    mid = rest.astype(BF16)
    low = (rest - mid.astype(F32)).astype(BF16)
    return jnp.concatenate([high, mid, low], axis=0)


def fold(x):
    n = x.shape[0] // 3
    return x[0:n] + (x[n : 2 * n] + x[2 * n :])


def moved(x, deal):
    return fold(jnp.dot(pieces(x), deal, preferred_element_type=F32))


E_LO, E_HI, N_LO, N_HI, V_LO, V_HI, DB_LO, DB_HI, S_LO, S_HI, LL, LH, HL, HH = range(14)


def kernel(
    dims,
    v_hbm,
    bg_hbm,
    d_hbm,
    e_hbm,
    n_hbm,
    c_hbm,
    out_ref,
    v_in,
    db_in,
    e_in,
    n_in,
    pad_e,
    pad_n,
    c_got,
    c_all,
    eg,
    e_all,
    ng,
    n_all,
    n_parts,
    e_halo,
    n_edge,
    n_halo,
    nat,
    side,
    db_halo,
    strip,
    strip_halo,
    corner_lo,
    corner_hi,
    deal_own,
    deal_side,
    panel,
    g_nat,
    b_nat,
    g_wide,
    b_wide,
    vel,
    mod,
    buoy,
    s_e,
    s_n,
    peak,
    flat,
    load_sem,
    send_sem,
    recv_sem,
):
    gx_n, gy_n, y_n, kx, ky = dims
    x_n = gy_n // y_n
    gx, gy = lax.axis_index("gx"), lax.axis_index("gy")
    outer, inner = gy // y_n, lax.rem(gy, y_n)
    lane = lane_index()
    rows = v_hbm.shape[1]
    half_rows = rows // 2
    modes = gy_n * ky

    def gxo(o):
        return lax.rem(gx + o + gx_n, gx_n)

    def gyo(o):
        return lax.rem(gy + o + gy_n, gy_n)

    def peer(e, d):
        return lax.rem(outer + e, x_n) * y_n + lax.rem(inner + d, y_n)

    mid_rows = rows - 2 * OFF
    bands = ((0, OFF), (rows - OFF, OFF), (OFF, mid_rows))
    moves = [(n_hbm, n_in), (d_hbm, db_in.at[0]), (bg_hbm, db_in.at[1])]
    moves += [(v_hbm.at[:, pl.ds(a, n)], v_in.at[:, pl.ds(a, n)]) for a, n in bands]
    moves += [(e_hbm, e_in), (c_hbm, c_got.at[0])]
    loads = [pltpu.make_async_copy(src, dst, load_sem.at[i]) for i, (src, dst) in enumerate(moves)]
    for load in loads:
        load.start()

    partners = [{"gx": gxo(a), "gy": gyo(b)} for a in (-1, 0, 1) for b in (-1, 0, 1) if a or b]
    partners += [{"gy": peer(0, d)} for d in range(1, y_n)]
    partners += [{"gy": peer(e, 0)} for e in range(1, x_n)]
    partners += [{"gx": gxo(o)} for o in range(1, gx_n)]
    barrier = pltpu.get_barrier_semaphore()
    for partner in partners:
        pl.semaphore_signal(barrier, inc=1, device_id=partner, device_id_type=MESH)

    sent = []

    def send(src, dst, slot, target):
        copy = pltpu.make_async_remote_copy(
            src_ref=src,
            dst_ref=dst,
            send_sem=send_sem.at[len(sent)],
            recv_sem=recv_sem.at[slot],
            device_id=target,
            device_id_type=MESH,
        )
        copy.start()
        sent.append(copy)

    def arrived(dst, slot):
        pltpu.make_async_copy(dst, dst, recv_sem.at[slot]).wait()

    c_base = 14
    e_base = c_base + gy_n
    n_base = e_base + gy_n

    pad_e[...] = jnp.zeros_like(pad_e)
    pad_n[...] = jnp.zeros_like(pad_n)
    e_all[...] = jnp.zeros_like(e_all)
    n_all[...] = jnp.zeros_like(n_all)

    pl.semaphore_wait(barrier, len(partners))

    send(e_hbm, e_halo.at[0], E_LO, {"gx": gxo(1)})
    send(e_hbm, e_halo.at[1], E_HI, {"gx": gxo(-1)})
    for d in range(1, y_n):
        send(c_hbm, c_got.at[d], c_base + d, {"gy": peer(0, d)})
    for e in range(1, x_n):
        send(c_hbm, c_got.at[e * y_n], c_base + e * y_n, {"gy": peer(e, 0)})

    loads[0].wait()
    pad_n[0:kx, :] = n_in[...]
    n0, n1 = (pad_n[0:SUB, 0:LANES], pad_n[0:SUB, LANES:]), (pad_n[SUB:, 0:LANES], pad_n[SUB:, LANES:])
    n_edge[0] = jnp.where(lane < HALO, n0[0], roll(n1[0], HALO))
    n_edge[1] = jnp.where(lane < HALO, roll(n0[1], HALO), roll(n1[1], 2 * HALO))
    send(n_edge.at[1], n_halo.at[0], N_LO, {"gy": gyo(1)})
    send(n_edge.at[0], n_halo.at[1], N_HI, {"gy": gyo(-1)})

    loads[1].wait()
    loads[2].wait()
    send(db_in.at[:, pl.ds(rows - OFF, OFF)], db_halo.at[0], DB_LO, {"gx": gxo(1)})
    send(db_in.at[:, pl.ds(0, OFF)], db_halo.at[1], DB_HI, {"gx": gxo(-1)})

    def lead(a):
        at = pl.multiple_of(a * SUB, SUB)
        for r in range(SUB):
            for t in range(2):
                nat[t, pl.ds((OFF + a * SUB) * SUB + r, SUB, stride=SUB), :] = v_in[
                    r, pl.ds(at, SUB), t * LANES : (t + 1) * LANES
                ]

    edge = HALO * SUB

    def own(first):
        return nat.at[:, pl.ds((OFF + first) * SUB, edge)]

    for k, (first, count) in enumerate(bands):
        loads[3 + k].wait()
        pl.loop(first // SUB, (first + count) // SUB)(lead)
        if k == 0:
            send(own(0), own(rows), V_HI, {"gx": gxo(-1)})
        if k == 1:
            send(own(rows - HALO), own(-HALO), V_LO, {"gx": gxo(1)})

    def tile(t, i):
        return nat[t, pl.ds(pl.multiple_of((OFF + i) * SUB, SUB), SUB), :]

    full = rows // PER

    def pack(g, count):
        low = jnp.zeros((SUB, LANES), F32)
        high = jnp.zeros((SUB, LANES), F32)
        for p in range(count):
            here = (lane >= p * HALO) & (lane < (p + 1) * HALO)
            low = jnp.where(here, roll(tile(0, g * PER + p), p * HALO), low)
            high = jnp.where(here, roll(tile(1, g * PER + p), (p + 1) * HALO), high)
        strip[0, 1 + g] = low
        strip[1, 1 + g] = high

    pl.loop(0, full)(lambda g: pack(g, PER))
    slabs = full
    if rows % PER:
        pack(full, rows % PER)
        slabs += 1
    hi_tile = rows // SUB - 3
    groups = ((0, range(0, 3)), (slabs + 1, range(hi_tile, hi_tile + 3)), (slabs + 2, range(3, hi_tile)))
    for slab, blocks in groups:
        low = jnp.zeros((SUB, LANES), F32)
        high = jnp.zeros((SUB, LANES), F32)
        for j, a in enumerate(blocks):
            for q in range(2):
                p = 2 * j + q
                here = (lane >= p * HALO) & (lane < (p + 1) * HALO)
                low = jnp.where(here, roll(db_in[q, a * SUB : (a + 1) * SUB, 0:LANES], p * HALO), low)
                high = jnp.where(here, roll(db_in[q, a * SUB : (a + 1) * SUB, LANES:], (p + 1) * HALO), high)
        strip[0, slab] = low
        strip[1, slab] = high
    first_hi = (rows - HALO) // PER
    lo_len, hi_len = corner_hi.shape[1], corner_lo.shape[1]
    lo_rows, hi_rows = pl.ds(0, lo_len), pl.ds(1 + first_hi, hi_len)
    send(strip.at[1], strip_halo.at[0], S_LO, {"gy": gyo(1)})
    send(strip.at[0], strip_halo.at[1], S_HI, {"gy": gyo(-1)})
    send(strip.at[1, hi_rows], corner_lo.at[0], LL, {"gx": gxo(1), "gy": gyo(1)})
    send(strip.at[0, hi_rows], corner_lo.at[1], LH, {"gx": gxo(1), "gy": gyo(-1)})
    send(strip.at[1, lo_rows], corner_hi.at[0], HL, {"gx": gxo(-1), "gy": gyo(1)})
    send(strip.at[0, lo_rows], corner_hi.at[1], HH, {"gx": gxo(-1), "gy": gyo(-1)})

    for half in range(2):
        for p in range(PLANES):
            for ref, n in ((deal_own, 2 * LANES), (deal_side, LANES)):
                k = lax.broadcasted_iota(jnp.int32, (n, LANES), 0)
                l = lax.broadcasted_iota(jnp.int32, (n, LANES), 1) - half * HALF
                if n == LANES:
                    index = jnp.where(k < HALO, k, jnp.where(k < 2 * HALO, k + 2 * LANES, -1))
                else:
                    index = k + HALO
                hit = (PLANES * l + p == index) & (l >= 0) & (l < HALF)
                ref[half * n : (half + 1) * n, p * LANES : (p + 1) * LANES] = jnp.where(hit, 1.0, 0.0).astype(BF16)

    loads[6].wait()
    arrived(e_halo.at[0], E_LO)
    arrived(e_halo.at[1], E_HI)
    for k, piece in enumerate((e_halo[0], e_in[...], e_halo[1])):
        pad_e[k, 0:ky, 0:rows] = piece
    eg[0] = jnp.where(
        lane < OFF,
        roll(pad_e[0], OFF - rows),
        jnp.where(lane < OFF + rows, roll(pad_e[1], OFF), roll(pad_e[2], OFF + rows)),
    )
    for d in range(1, y_n):
        send(eg.at[0], eg.at[d], e_base + d, {"gy": peer(0, d)})
    for e in range(1, x_n):
        send(eg.at[0], eg.at[e * y_n], e_base + e * y_n, {"gy": peer(e, 0)})
    arrived(n_halo.at[0], N_LO)
    arrived(n_halo.at[1], N_HI)

    def flank(west, east):
        return jnp.where(lane < HALO, west, jnp.where(lane < 2 * HALO, east, 0.0))

    for half, (t0, t1) in enumerate((n0, n1)):
        beside = flank(roll(n_halo[0], -half * HALO), roll(n_halo[1], (1 - half) * HALO))
        for t, value in enumerate((t0, t1, beside)):
            ng[gx, t, half * SUB : (half + 1) * SUB, :] = value
    for o in range(1, gx_n):
        send(ng.at[gx], ng.at[gx], n_base + o, {"gx": gxo(o)})

    for d in sorted(range(1, y_n), key=lambda d: min(d, y_n - d)):
        arrived(c_got.at[d], c_base + d)
        for e in range(1, x_n):
            send(c_got.at[d], c_got.at[e * y_n + d], c_base + e * y_n + d, {"gy": peer(e, 0)})
        arrived(eg.at[d], e_base + d)
        for e in range(1, x_n):
            send(eg.at[d], eg.at[e * y_n + d], e_base + e * y_n + d, {"gy": peer(e, 0)})

    one = jnp.float32(1.0)
    west_gain, east_gain = jnp.where(gy > 0, one, 0.0), jnp.where(gy < gy_n - 1, one, 0.0)
    low_gain, high_gain = jnp.where(gx > 0, one, 0.0), jnp.where(gx < gx_n - 1, one, 0.0)

    arrived(strip_halo.at[0], S_LO)
    arrived(strip_halo.at[1], S_HI)

    def unpack(west, east, p):
        return flank(roll(west, -p * HALO) * west_gain, roll(east, (1 - p) * HALO) * east_gain)

    def own_sides(g, count):
        for p in range(count):
            at = pl.multiple_of((OFF + g * PER + p) * SUB, SUB)
            side[pl.ds(at, SUB), :] = unpack(strip_halo[0, 1 + g], strip_halo[1, 1 + g], p)

    pl.loop(0, full)(lambda g: own_sides(g, PER))
    if rows % PER:
        own_sides(full, rows % PER)

    arrived(own(-HALO), V_LO)
    arrived(own(rows), V_HI)
    for s, slot in ((0, LL), (1, LH)):
        arrived(corner_lo.at[s], slot)
    for s, slot in ((0, HL), (1, HH)):
        arrived(corner_hi.at[s], slot)
    for i in range(HALO):
        for corner, row, at, slab, gain in (
            (corner_lo, rows - HALO + i, OFF - HALO + i, (rows - HALO + i) // PER - first_hi, low_gain),
            (corner_hi, i, OFF + rows + i, 1 + i // PER, high_gain),
        ):
            here = slice(at * SUB, (at + 1) * SUB)
            side[here, :] = unpack(corner[0, slab], corner[1, slab], row % PER) * gain
            for t in range(2):
                nat[t, here, :] = nat[t, here, :] * gain

    def dealt(natural, first, count, apart):
        near, far = pl.ds(first, count), pl.ds(first + apart, count)
        wide = jnp.concatenate([natural(t, at) for at in (near, far) for t in range(2)], axis=1)
        sides = jnp.concatenate([natural(2, at) for at in (near, far)], axis=1)
        return fold(
            jnp.dot(pieces(wide), deal_own[...], preferred_element_type=F32)
            + jnp.dot(pieces(sides), deal_side[...], preferred_element_type=F32)
        )

    wide_rows = vel.shape[1]
    chunk = 16

    @pl.loop(0, wide_rows // chunk)
    def _(c):
        first = pl.multiple_of(c * chunk * SUB, chunk * SUB)
        out = dealt(lambda t, at: nat[t, at, :] if t < 2 else side[at, :], first, chunk * SUB, half_rows * SUB)
        for u in range(chunk):
            for p in range(PLANES):
                vel[p, c * chunk + u] = out[u * SUB : (u + 1) * SUB, p * LANES : (p + 1) * LANES]

    for s, slot in ((0, DB_LO), (1, DB_HI)):
        arrived(db_halo.at[s], slot)
    tiles = rows // SUB
    for b in range(tiles + 6):
        values = []
        for q in range(2):
            if b < 3:
                body, a = db_halo.at[0, q], b
                w, e = (corner_lo[s, hi_len - 1] for s in range(2))
                p = 2 * b + q
            elif b < tiles + 3:
                body, a = db_in.at[q], b - 3
                slab, blocks = next(g for g in groups if a in g[1])
                w, e = (strip_halo[s, slab] for s in range(2))
                p = 2 * (a - blocks[0]) + q
            else:
                body, a = db_halo.at[1, q], b - 3 - tiles
                w, e = (corner_hi[s, 0] for s in range(2))
                p = 2 * a + q
            t0, t1 = (body[a * SUB : (a + 1) * SUB, t * LANES : (t + 1) * LANES] for t in range(2))
            values.append((t0, t1, flank(roll(w, -p * HALO), roll(e, (1 - p) * HALO))))
        gain = low_gain if b < 3 else high_gain if b >= tiles + 3 else one
        here = slice(b * SUB, (b + 1) * SUB)
        for t in range(3):
            d, s = values[0][t], values[1][t]
            keep = SCALE * gain
            if t == 2:
                keep = jnp.where(lane < HALO, west_gain, east_gain) * keep
                d = jnp.where(lane < 2 * HALO, d, 1.0)
            g_nat[t, here, :] = keep * d * s * s
            b_nat[t, here, :] = keep / d
    for natural, out in ((g_nat, g_wide), (b_nat, b_wide)):
        out[...] = dealt(lambda t, at, natural=natural: natural[t, at, :], 0, wide_rows, half_rows)

    for slot in range(y_n, gy_n):
        arrived(c_got.at[slot], c_base + slot)
        arrived(eg.at[slot], e_base + slot)
    loads[7].wait()
    c_all[...] = jnp.zeros_like(c_all)
    for slot in range(gy_n):
        e_all[slot * ky : (slot + 1) * ky, :] = eg[slot, 0:ky, :]
        for k in range(ky):
            at = (slot * ky + k) * SUB
            c_all[at : at + SUB, 0 : c_got.shape[3]] = c_got[slot, k]
    nat_rows = OFF + rows + OFF
    lhs = jnp.transpose(e_all[...])[0:nat_rows, 0:modes]
    for r in range(SUB):
        rhs = c_all[pl.ds(r, modes, stride=SUB), :]
        panel[pl.ds(r, nat_rows, stride=SUB), :] = jnp.dot(
            lhs, rhs, precision=lax.Precision.HIGHEST, preferred_element_type=F32
        )

    for o in range(1, gx_n):
        at = gxo(-o)
        arrived(ng.at[at], n_base + o)
    for b in range(gx_n):
        for t in range(3):
            n_all[b * kx : (b + 1) * kx, t * LANES : (t + 1) * LANES] = ng[b, t, 0:kx, :]
    split = pieces(n_all[...])
    lower = jnp.dot(split[:, 0 : 2 * LANES], deal_own[0 : 2 * LANES, :], preferred_element_type=F32)
    lower += jnp.dot(split[:, 2 * LANES :], deal_side[0:LANES, :], preferred_element_type=F32)
    for p in range(PLANES):
        at = slice(p * LANES, (p + 1) * LANES)
        for j in range(3):
            part = lower[j * LANES : (j + 1) * LANES, at]
            n_parts[j, 0:LANES, at] = part.astype(BF16)
            n_parts[j, LANES:, at] = roll(part, HALF).astype(BF16)

    @pl.loop(0, wide_rows // chunk)
    def _(c):
        n = chunk * SUB
        near = pl.ds(pl.multiple_of(c * n, n), n)
        far = pl.ds(pl.multiple_of(c * n + half_rows * SUB, SUB), n)
        left = pieces(jnp.concatenate([panel[near, :], panel[far, :]], axis=1))
        a = jnp.dot(left, n_parts[0], preferred_element_type=F32)
        b = jnp.dot(left[0 : 2 * n], n_parts[1], preferred_element_type=F32)
        field = a[0:n] + (
            (a[n : 2 * n] + b[0:n])
            + (a[2 * n :] + b[n:] + jnp.dot(left[0:n], n_parts[2], preferred_element_type=F32))
        )
        for p in range(PLANES):
            at = slice(p * LANES, (p + 1) * LANES)
            first = pl.multiple_of(c * chunk, chunk)
            g, w = g_wide[pl.ds(first, chunk), at], b_wide[pl.ds(first, chunk), at]
            for u in range(chunk):
                q = 1.0 + GAIN * jnp.tanh(field[u * SUB : (u + 1) * SUB, at])
                mod[p, c * chunk + u] = jnp.broadcast_to(g[u : u + 1], (SUB, LANES)) * (q * q)
                buoy[p, c * chunk + u] = jnp.broadcast_to(w[u : u + 1], (SUB, LANES))

    zero = jnp.zeros((SUB, LANES), F32)
    for step in range(1, STEPS + 1):
        begin = OFF - HALO + 3 * step - 2
        count = half_rows + 2 * HALO + 3 - 6 * step
        chunks = -(-count // UNROLL)

        def sweep(c, carry, begin=begin, first=step == 1):
            carry = list(carry)
            for u in range(UNROLL):
                i = begin + c * UNROLL + u
                v0 = [carry[p][1] for p in range(PLANES)]
                n1_ = [carry[p][6] for p in range(PLANES)]
                v0 += [roll(v0[0], -1), roll(v0[1], -1), roll(v0[-1], 1)]
                n1_ += [roll(n1_[0], -1), roll(n1_[-2], 1), roll(n1_[-1], 1)]
                for p in range(PLANES):
                    vm, _, v1, e3, e2, e1, _ = carry[p]
                    v2 = vel[p, i + 2]
                    m = mod[p, i]
                    ge = 27.0 * (v1 - v0[p]) - (v2 - vm)
                    gn = 27.0 * (v0[p + 1] - v0[p]) - (v0[p + 2] - v0[p - 1])
                    se, sn = m * ge, m * gn
                    if not first:
                        se, sn = s_e[p, i] + se, s_n[p, i] + sn
                    if step < STEPS:
                        s_e[p, i] = se
                        s_n[p, i] = sn
                    near = (e1 - e2) + (n1_[p] - n1_[p - 1])
                    far = (se - e3) + (n1_[p + 1] - n1_[p - 2])
                    vn = vm + buoy[p, i - 1] * (27.0 * near - far)
                    if step < STEPS:
                        vel[p, i - 1] = vn
                    top = jnp.abs(vn)
                    peak[p, i - 1] = top if first else jnp.maximum(peak[p, i - 1], top)
                    carry[p] = (v0[p], v1, v2, e2, e1, se, sn)
            return tuple(carry)

        start = tuple(
            (vel[p, begin - 1], vel[p, begin], vel[p, begin + 1], zero, zero, zero, zero) for p in range(PLANES)
        )
        lax.fori_loop(0, chunks, sweep, start)

    @pl.loop(0, half_rows // SUB)
    def _(a):
        at = pl.multiple_of(a * SUB, SUB)
        block = jnp.concatenate(
            [
                jnp.concatenate([peak[p, OFF + a * SUB + u] for u in range(SUB)], axis=0)
                for p in range(PLANES)
            ],
            axis=1,
        )
        back = fold(
            lax.dot_general(
                pieces(block), deal_own[...], (((1,), (1,)), ((), ())), preferred_element_type=F32
            )
        )
        for t in range(4):
            flat[t] = back[:, t * LANES : (t + 1) * LANES]
            upper = pl.multiple_of(at + (t // 2) * half_rows, SUB)
            for r in range(SUB):
                out_ref[r, pl.ds(upper, SUB), (t % 2) * LANES : (t % 2 + 1) * LANES] = flat[
                    t, pl.ds(r, SUB, stride=SUB), :
                ]

    for copy in sent:
        copy.wait_send()


def on_device(gx_n, gy_n, initial_velocity, background_speed, density, east_modes, north_modes, mode_coef):
    reals, rows, cols = initial_velocity.shape
    kx, ky = north_modes.shape[0], east_modes.shape[1]
    y_n = 4 if gy_n == 16 else 2
    x_n = gy_n // y_n
    wide = rows // 2 + 2 * OFF
    natural = rows + 2 * OFF
    slabs = -(-rows // PER)
    lo_len = 1 + (HALO - 1) // PER + 1
    hi_len = slabs - (rows - HALO) // PER + 1
    sends = 4 + 2 + 2 + 2 + 4 + 2 * (gy_n - 1) + gx_n - 1
    vmem = lambda *shape: pltpu.VMEM(shape, F32)
    scratch = [
        vmem(reals, rows, cols),
        vmem(2, rows, cols),
        vmem(ky, rows),
        vmem(kx, cols),
        vmem(3, SUB, LANES),
        vmem(16, cols),
        vmem(gy_n, ky, reals, mode_coef.shape[2]),
        vmem(gy_n * ky * reals, LANES),
        vmem(gy_n, SUB, LANES),
        vmem(LANES, LANES),
        vmem(gx_n, 3, 16, LANES),
        vmem(LANES, 3 * LANES),
        pltpu.VMEM((3, 2 * LANES, WIDE), BF16),
        vmem(2, ky, rows),
        vmem(2, SUB, LANES),
        vmem(2, SUB, LANES),
        vmem(2, natural * SUB, LANES),
        vmem(natural * SUB, LANES),
        vmem(2, 2, OFF, cols),
        vmem(2, slabs + 3, SUB, LANES),
        vmem(2, slabs + 3, SUB, LANES),
        vmem(2, hi_len, SUB, LANES),
        vmem(2, lo_len, SUB, LANES),
        pltpu.VMEM((4 * LANES, WIDE), BF16),
        pltpu.VMEM((2 * LANES, WIDE), BF16),
        vmem(natural * SUB, LANES),
        vmem(3, natural, LANES),
        vmem(3, natural, LANES),
        vmem(wide, WIDE),
        vmem(wide, WIDE),
        vmem(PLANES, wide, SUB, LANES),
        vmem(PLANES, wide, SUB, LANES),
        vmem(PLANES, wide, SUB, LANES),
        vmem(PLANES, wide, SUB, LANES),
        vmem(PLANES, wide, SUB, LANES),
        vmem(PLANES, wide, SUB, LANES),
        vmem(4, SUB * SUB, LANES),
        pltpu.SemaphoreType.DMA((8,)),
        pltpu.SemaphoreType.DMA((sends,)),
        pltpu.SemaphoreType.DMA((14 + 2 * gy_n + gx_n,)),
    ]
    return pl.pallas_call(
        functools.partial(kernel, (gx_n, gy_n, y_n, kx, ky)),
        out_shape=jax.ShapeDtypeStruct(initial_velocity.shape, F32),
        in_specs=[pl.BlockSpec(memory_space=pl.ANY)] * 6,
        out_specs=pl.BlockSpec(memory_space=pltpu.VMEM),
        scratch_shapes=scratch,
        compiler_params=pltpu.CompilerParams(
            collective_id=0, has_side_effects=True, vmem_limit_bytes=60 * 1024 * 1024
        ),
    )(
        initial_velocity,
        background_speed,
        density,
        jnp.transpose(east_modes),
        north_modes,
        jnp.transpose(mode_coef, (1, 0, 2)),
    )


def solution(mesh):
    in_specs = (
        P("row", "gx", "gy"),
        P("gx", "gy"),
        P("gx", "gy"),
        P("gx", "gy"),
        P("gx", "gy"),
        P("row", "gy", None),
    )
    out_specs = P("row", "gx", "gy")
    body = functools.partial(on_device, mesh.shape["gx"], mesh.shape["gy"])
    return jax.shard_map(body, mesh=mesh, in_specs=in_specs, out_specs=out_specs, check_vma=False)
```

```python
import functools

import jax
import jax.numpy as jnp
from jax import lax
from jax.experimental import pallas as pl
from jax.experimental.pallas import tpu as pltpu
from jax.sharding import PartitionSpec as P

MESH = pl.DeviceIdType.MESH
F32 = jnp.float32
STEPS = 6
HALO = 3 * STEPS
OFF = 24
LANES = 128
SUB = 8
PER = LANES // HALO
PLANES = 5
HALF = LANES // 2
WIDE = PLANES * LANES
BF16 = jnp.bfloat16
SCALE = 0.55 / 24.0
GAIN = 0.03


def roll(x, shift, axis=1):
    shift %= x.shape[axis]
    return pltpu.roll(x, shift, axis) if shift else x


def lane_index():
    return lax.broadcasted_iota(jnp.int32, (SUB, LANES), 1)


def pieces(x, count):
    parts = []
    for _ in range(count):
        parts.append(x.astype(BF16))
        x = x - parts[-1].astype(F32)
    return jnp.concatenate(parts, axis=0)


def fold(x):
    n = x.shape[0] // 2
    return x[0:n] + x[n:]


E_LO, E_HI, N_LO, N_HI, V_LO, V_HI, D_LO, D_HI, B_LO, B_HI, S_LO, S_HI, LL, LH, HL, HH = range(16)


def kernel(
    dims,
    v_hbm,
    bg_hbm,
    d_hbm,
    e_hbm,
    n_hbm,
    c_hbm,
    out_ref,
    v_in,
    db_in,
    e_in,
    n_in,
    pad_e,
    pad_n,
    c_got,
    c_all,
    eg,
    e_all,
    ng,
    n_all,
    n_parts,
    e_halo,
    n_edge,
    n_halo,
    nat,
    side,
    db_halo,
    strip,
    strip_halo,
    corner_lo,
    corner_hi,
    deal_own,
    deal_side,
    panel,
    g_nat,
    b_nat,
    g_wide,
    b_wide,
    vel,
    mod,
    buoy,
    s_e,
    s_n,
    peak,
    flat,
    load_sem,
    send_sem,
    recv_sem,
):
    gx_n, gy_n, y_n, kx, ky = dims
    x_n = gy_n // y_n
    gx, gy = lax.axis_index("gx"), lax.axis_index("gy")
    outer, inner = gy // y_n, lax.rem(gy, y_n)
    lane = lane_index()
    rows = v_hbm.shape[1]
    half_rows = rows // 2
    modes = gy_n * ky

    def gxo(o):
        return lax.rem(gx + o + gx_n, gx_n)

    def gyo(o):
        return lax.rem(gy + o + gy_n, gy_n)

    def peer(e, d):
        return lax.rem(outer + e, x_n) * y_n + lax.rem(inner + d, y_n)

    mid_rows = rows - 2 * OFF
    bands = ((0, OFF), (rows - OFF, OFF), (OFF, mid_rows))
    moves = [(n_hbm, n_in), (d_hbm, db_in.at[0]), (bg_hbm, db_in.at[1])]
    moves += [(v_hbm.at[:, pl.ds(a, n)], v_in.at[:, pl.ds(a, n)]) for a, n in bands]
    moves += [(e_hbm, e_in), (c_hbm, c_got.at[0])]
    loads = [pltpu.make_async_copy(src, dst, load_sem.at[i]) for i, (src, dst) in enumerate(moves)]
    for load in loads:
        load.start()

    partners = [{"gx": gxo(a), "gy": gyo(b)} for a in (-1, 0, 1) for b in (-1, 0, 1) if a or b]
    partners += [{"gy": peer(0, d)} for d in range(1, y_n)]
    partners += [{"gy": peer(e, 0)} for e in range(1, x_n)]
    partners += [{"gx": gxo(o)} for o in range(1, gx_n)]
    barrier = pltpu.get_barrier_semaphore()
    for partner in partners:
        pl.semaphore_signal(barrier, inc=1, device_id=partner, device_id_type=MESH)

    sent = []

    def send(src, dst, slot, target):
        copy = pltpu.make_async_remote_copy(
            src_ref=src,
            dst_ref=dst,
            send_sem=send_sem.at[len(sent)],
            recv_sem=recv_sem.at[slot],
            device_id=target,
            device_id_type=MESH,
        )
        copy.start()
        sent.append(copy)

    def arrived(dst, slot):
        pltpu.make_async_copy(dst, dst, recv_sem.at[slot]).wait()

    c_base = 16
    e_base = c_base + gy_n
    n_base = e_base + gy_n

    pad_e[...] = jnp.zeros_like(pad_e)
    pad_n[...] = jnp.zeros_like(pad_n)
    e_all[...] = jnp.zeros_like(e_all)
    n_all[...] = jnp.zeros_like(n_all)

    pl.semaphore_wait(barrier, len(partners))

    send(e_hbm, e_halo.at[0], E_LO, {"gx": gxo(1)})
    send(e_hbm, e_halo.at[1], E_HI, {"gx": gxo(-1)})
    for d in range(1, y_n):
        send(c_hbm, c_got.at[d], c_base + d, {"gy": peer(0, d)})
    for e in range(1, x_n):
        send(c_hbm, c_got.at[e * y_n], c_base + e * y_n, {"gy": peer(e, 0)})

    for src, lo, hi, q in ((d_hbm, D_LO, D_HI, 0), (bg_hbm, B_LO, B_HI, 1)):
        send(src.at[pl.ds(rows - OFF, OFF)], db_halo.at[0, q], lo, {"gx": gxo(1)})
        send(src.at[pl.ds(0, OFF)], db_halo.at[1, q], hi, {"gx": gxo(-1)})

    loads[0].wait()
    pad_n[0:kx, :] = n_in[...]
    n0, n1 = (pad_n[0:SUB, 0:LANES], pad_n[0:SUB, LANES:]), (pad_n[SUB:, 0:LANES], pad_n[SUB:, LANES:])
    n_edge[0] = jnp.where(lane < HALO, n0[0], roll(n1[0], HALO))
    n_edge[1] = jnp.where(lane < HALO, roll(n0[1], HALO), roll(n1[1], 2 * HALO))
    send(n_edge.at[1], n_halo.at[0], N_LO, {"gy": gyo(1)})
    send(n_edge.at[0], n_halo.at[1], N_HI, {"gy": gyo(-1)})

    def lead(a):
        at = pl.multiple_of(a * SUB, SUB)
        for r in range(SUB):
            for t in range(2):
                nat[t, pl.ds((OFF + a * SUB) * SUB + r, SUB, stride=SUB), :] = v_in[
                    r, pl.ds(at, SUB), t * LANES : (t + 1) * LANES
                ]

    edge = HALO * SUB

    def own(first):
        return nat.at[:, pl.ds((OFF + first) * SUB, edge)]

    for k, (first, count) in enumerate(bands):
        loads[3 + k].wait()
        pl.loop(first // SUB, (first + count) // SUB)(lead)
        if k == 0:
            send(own(0), own(rows), V_HI, {"gx": gxo(-1)})
        if k == 1:
            send(own(rows - HALO), own(-HALO), V_LO, {"gx": gxo(1)})

    loads[1].wait()
    loads[2].wait()

    def tile(t, i):
        return nat[t, pl.ds(pl.multiple_of((OFF + i) * SUB, SUB), SUB), :]

    full = rows // PER

    def pack(g, count):
        low = jnp.zeros((SUB, LANES), F32)
        high = jnp.zeros((SUB, LANES), F32)
        for p in range(count):
            here = (lane >= p * HALO) & (lane < (p + 1) * HALO)
            low = jnp.where(here, roll(tile(0, g * PER + p), p * HALO), low)
            high = jnp.where(here, roll(tile(1, g * PER + p), (p + 1) * HALO), high)
        strip[0, 1 + g] = low
        strip[1, 1 + g] = high

    pl.loop(0, full)(lambda g: pack(g, PER))
    slabs = full
    if rows % PER:
        pack(full, rows % PER)
        slabs += 1
    hi_tile = rows // SUB - 3
    groups = ((0, range(0, 3)), (slabs + 1, range(hi_tile, hi_tile + 3)), (slabs + 2, range(3, hi_tile)))
    for slab, blocks in groups:
        low = jnp.zeros((SUB, LANES), F32)
        high = jnp.zeros((SUB, LANES), F32)
        for j, a in enumerate(blocks):
            for q in range(2):
                p = 2 * j + q
                here = (lane >= p * HALO) & (lane < (p + 1) * HALO)
                low = jnp.where(here, roll(db_in[q, a * SUB : (a + 1) * SUB, 0:LANES], p * HALO), low)
                high = jnp.where(here, roll(db_in[q, a * SUB : (a + 1) * SUB, LANES:], (p + 1) * HALO), high)
        strip[0, slab] = low
        strip[1, slab] = high
    first_hi = (rows - HALO) // PER
    lo_len, hi_len = corner_hi.shape[1], corner_lo.shape[1]
    lo_rows, hi_rows = pl.ds(0, lo_len), pl.ds(1 + first_hi, hi_len)
    send(strip.at[1], strip_halo.at[0], S_LO, {"gy": gyo(1)})
    send(strip.at[0], strip_halo.at[1], S_HI, {"gy": gyo(-1)})
    send(strip.at[1, hi_rows], corner_lo.at[0], LL, {"gx": gxo(1), "gy": gyo(1)})
    send(strip.at[0, hi_rows], corner_lo.at[1], LH, {"gx": gxo(1), "gy": gyo(-1)})
    send(strip.at[1, lo_rows], corner_hi.at[0], HL, {"gx": gxo(-1), "gy": gyo(1)})
    send(strip.at[0, lo_rows], corner_hi.at[1], HH, {"gx": gxo(-1), "gy": gyo(-1)})

    loads[6].wait()
    arrived(e_halo.at[0], E_LO)
    arrived(e_halo.at[1], E_HI)
    for k, piece in enumerate((e_halo[0], e_in[...], e_halo[1])):
        pad_e[k, 0:ky, 0:rows] = piece
    eg[0] = jnp.where(
        lane < OFF,
        roll(pad_e[0], OFF - rows),
        jnp.where(lane < OFF + rows, roll(pad_e[1], OFF), roll(pad_e[2], OFF + rows)),
    )
    for d in range(1, y_n):
        send(eg.at[0], eg.at[d], e_base + d, {"gy": peer(0, d)})
    for e in range(1, x_n):
        send(eg.at[0], eg.at[e * y_n], e_base + e * y_n, {"gy": peer(e, 0)})
    arrived(n_halo.at[0], N_LO)
    arrived(n_halo.at[1], N_HI)

    def flank(west, east):
        return jnp.where(lane < HALO, west, jnp.where(lane < 2 * HALO, east, 0.0))

    for half, (t0, t1) in enumerate((n0, n1)):
        beside = flank(roll(n_halo[0], -half * HALO), roll(n_halo[1], (1 - half) * HALO))
        for t, value in enumerate((t0, t1, beside)):
            ng[gx, t, half * SUB : (half + 1) * SUB, :] = value
    for o in range(1, gx_n):
        send(ng.at[gx], ng.at[gx], n_base + o, {"gx": gxo(o)})

    for d in sorted(range(1, y_n), key=lambda d: min(d, y_n - d)):
        arrived(c_got.at[d], c_base + d)
        for e in range(1, x_n):
            send(c_got.at[d], c_got.at[e * y_n + d], c_base + e * y_n + d, {"gy": peer(e, 0)})
        arrived(eg.at[d], e_base + d)
        for e in range(1, x_n):
            send(eg.at[d], eg.at[e * y_n + d], e_base + e * y_n + d, {"gy": peer(e, 0)})

    for half in range(2):
        for p in range(PLANES):
            for ref, n in ((deal_own, 2 * LANES), (deal_side, LANES)):
                k = lax.broadcasted_iota(jnp.int32, (n, LANES), 0)
                l = lax.broadcasted_iota(jnp.int32, (n, LANES), 1) - half * HALF
                if n == LANES:
                    index = jnp.where(k < HALO, k, jnp.where(k < 2 * HALO, k + 2 * LANES, -1))
                else:
                    index = k + HALO
                hit = (PLANES * l + p == index) & (l >= 0) & (l < HALF)
                ref[half * n : (half + 1) * n, p * LANES : (p + 1) * LANES] = jnp.where(hit, 1.0, 0.0).astype(BF16)

    one = jnp.float32(1.0)
    west_gain, east_gain = jnp.where(gy > 0, one, 0.0), jnp.where(gy < gy_n - 1, one, 0.0)
    low_gain, high_gain = jnp.where(gx > 0, one, 0.0), jnp.where(gx < gx_n - 1, one, 0.0)

    arrived(strip_halo.at[0], S_LO)
    arrived(strip_halo.at[1], S_HI)

    def unpack(west, east, p):
        return flank(roll(west, -p * HALO) * west_gain, roll(east, (1 - p) * HALO) * east_gain)

    def own_sides(g, count):
        for p in range(count):
            at = pl.multiple_of((OFF + g * PER + p) * SUB, SUB)
            side[pl.ds(at, SUB), :] = unpack(strip_halo[0, 1 + g], strip_halo[1, 1 + g], p)

    pl.loop(0, full)(lambda g: own_sides(g, PER))
    if rows % PER:
        own_sides(full, rows % PER)

    def dealt(natural, firsts, count, apart):
        def tiles(ts, shift):
            return jnp.concatenate(
                [jnp.concatenate([natural(t, pl.ds(f + shift, count)) for t in ts], axis=1) for f in firsts], axis=0
            )

        wide = jnp.concatenate([tiles((0, 1), 0), tiles((0, 1), apart)], axis=1)
        sides = jnp.concatenate([tiles((2,), 0), tiles((2,), apart)], axis=1)
        return fold(
            jnp.dot(pieces(wide, 2), deal_own[...], preferred_element_type=F32)
            + jnp.dot(pieces(sides, 2), deal_side[...], preferred_element_type=F32)
        )

    def deal_velocity(firsts, count):
        out = dealt(
            lambda t, at: nat[t, at, :] if t < 2 else side[at, :],
            [f * SUB for f in firsts],
            count * SUB,
            half_rows * SUB,
        )
        for k, f in enumerate(firsts):
            for u in range(count):
                for p in range(PLANES):
                    at = (k * count + u) * SUB
                    vel[p, f + u] = out[at : at + SUB, p * LANES : (p + 1) * LANES]

    wide_rows = vel.shape[1]
    deal_velocity([OFF], half_rows)

    for s in range(2):
        for q in range(2):
            arrived(db_halo.at[s, q], (D_LO, D_HI, B_LO, B_HI)[2 * q + s])
    for s, slot in ((0, LL), (1, LH)):
        arrived(corner_lo.at[s], slot)
    for s, slot in ((0, HL), (1, HH)):
        arrived(corner_hi.at[s], slot)
    tiles = rows // SUB
    for b in range(tiles + 6):
        values = []
        for q in range(2):
            if b < 3:
                body, a = db_halo.at[0, q], b
                w, e = (corner_lo[s, hi_len - 1] for s in range(2))
                p = 2 * b + q
            elif b < tiles + 3:
                body, a = db_in.at[q], b - 3
                slab, blocks = next(g for g in groups if a in g[1])
                w, e = (strip_halo[s, slab] for s in range(2))
                p = 2 * (a - blocks[0]) + q
            else:
                body, a = db_halo.at[1, q], b - 3 - tiles
                w, e = (corner_hi[s, 0] for s in range(2))
                p = 2 * a + q
            t0, t1 = (body[a * SUB : (a + 1) * SUB, t * LANES : (t + 1) * LANES] for t in range(2))
            values.append((t0, t1, flank(roll(w, -p * HALO), roll(e, (1 - p) * HALO))))
        gain = low_gain if b < 3 else high_gain if b >= tiles + 3 else one
        here = slice(b * SUB, (b + 1) * SUB)
        for t in range(3):
            d, s = values[0][t], values[1][t]
            keep = SCALE * gain
            if t == 2:
                keep = jnp.where(lane < HALO, west_gain, east_gain) * keep
                d = jnp.where(lane < 2 * HALO, d, 1.0)
            g_nat[t, here, :] = keep * d * s * s
            b_nat[t, here, :] = keep / d
    for natural, out in ((g_nat, g_wide), (b_nat, b_wide)):
        out[...] = dealt(lambda t, at, natural=natural: natural[t, at, :], [0], wide_rows, half_rows)

    for slot in range(y_n, gy_n):
        arrived(c_got.at[slot], c_base + slot)
        arrived(eg.at[slot], e_base + slot)
    loads[7].wait()
    c_all[...] = jnp.zeros_like(c_all)
    for slot in range(gy_n):
        e_all[slot * ky : (slot + 1) * ky, :] = eg[slot, 0:ky, :]
        for k in range(ky):
            at = (slot * ky + k) * SUB
            c_all[at : at + SUB, 0 : c_got.shape[3]] = c_got[slot, k]
    nat_rows = OFF + rows + OFF
    lhs = jnp.transpose(e_all[...])[0:nat_rows, 0:modes]
    for r in range(SUB):
        rhs = c_all[pl.ds(r, modes, stride=SUB), :]
        panel[pl.ds(r, nat_rows, stride=SUB), :] = jnp.dot(
            lhs, rhs, precision=lax.Precision.HIGHEST, preferred_element_type=F32
        )

    for o in range(1, gx_n):
        at = gxo(-o)
        arrived(ng.at[at], n_base + o)
    for b in range(gx_n):
        for t in range(3):
            n_all[b * kx : (b + 1) * kx, t * LANES : (t + 1) * LANES] = ng[b, t, 0:kx, :]
    split = pieces(n_all[...], 3)
    lower = jnp.dot(split[:, 0 : 2 * LANES], deal_own[0 : 2 * LANES, :], preferred_element_type=F32)
    lower += jnp.dot(split[:, 2 * LANES :], deal_side[0:LANES, :], preferred_element_type=F32)
    for p in range(PLANES):
        at = slice(p * LANES, (p + 1) * LANES)
        for j in range(3):
            part = lower[j * LANES : (j + 1) * LANES, at]
            n_parts[j, 0:LANES, at] = part.astype(BF16)
            n_parts[j, LANES:, at] = roll(part, HALF).astype(BF16)

    begin = OFF - HALO
    chunk = half_rows // 2 + HALO
    for c in range(2):
        n = chunk * SUB
        first = begin + c * chunk
        near, far = (slice((first + a) * SUB, (first + a) * SUB + n) for a in (0, half_rows))
        left = pieces(jnp.concatenate([panel[near, :], panel[far, :]], axis=1), 3)
        a = jnp.dot(left, n_parts[0], preferred_element_type=F32)
        b = jnp.dot(left[0 : 2 * n], n_parts[1], preferred_element_type=F32)
        field = a[0:n] + (
            (a[n : 2 * n] + b[0:n])
            + (a[2 * n :] + b[n:] + jnp.dot(left[0:n], n_parts[2], preferred_element_type=F32))
        )
        for p in range(PLANES):
            at = slice(p * LANES, (p + 1) * LANES)
            g, w = g_wide[first : first + chunk, at], b_wide[first : first + chunk, at]
            for u in range(chunk):
                q = 1.0 + GAIN * jnp.tanh(field[u * SUB : (u + 1) * SUB, at])
                mod[p, first + u] = jnp.broadcast_to(g[u : u + 1], (SUB, LANES)) * (q * q)
                buoy[p, first + u] = jnp.broadcast_to(w[u : u + 1], (SUB, LANES))

    arrived(own(-HALO), V_LO)
    arrived(own(rows), V_HI)
    for i in range(HALO):
        for corner, row, at, slab, gain in (
            (corner_lo, rows - HALO + i, OFF - HALO + i, (rows - HALO + i) // PER - first_hi, low_gain),
            (corner_hi, i, OFF + rows + i, 1 + i // PER, high_gain),
        ):
            here = slice(at * SUB, (at + 1) * SUB)
            side[here, :] = unpack(corner[0, slab], corner[1, slab], row % PER) * gain
            for t in range(2):
                nat[t, here, :] = nat[t, here, :] * gain

    deal_velocity([0, OFF + half_rows], OFF)

    zero = jnp.zeros((SUB, LANES), F32)
    for step in range(1, STEPS + 1):
        begin = OFF - HALO + 3 * step - 2
        count = half_rows + 2 * HALO + 3 - 6 * step
        unroll = min(range(11, 15), key=lambda n: -count % n)
        chunks = -(-count // unroll)

        def sweep(c, carry, begin=begin, unroll=unroll, first=step == 1):
            carry = list(carry)
            for u in range(unroll):
                i = begin + c * unroll + u
                v0 = [carry[p][1] for p in range(PLANES)]
                n1_ = [carry[p][6] for p in range(PLANES)]
                v0 += [roll(v0[0], -1), roll(v0[1], -1), roll(v0[-1], 1)]
                n1_ += [roll(n1_[0], -1), roll(n1_[-2], 1), roll(n1_[-1], 1)]
                for p in range(PLANES):
                    vm, _, v1, e3, e2, e1, _ = carry[p]
                    v2 = vel[p, i + 2]
                    m = mod[p, i]
                    ge = 27.0 * (v1 - v0[p]) - (v2 - vm)
                    gn = 27.0 * (v0[p + 1] - v0[p]) - (v0[p + 2] - v0[p - 1])
                    se, sn = m * ge, m * gn
                    if not first:
                        se, sn = s_e[p, i] + se, s_n[p, i] + sn
                    if step < STEPS:
                        s_e[p, i] = se
                        s_n[p, i] = sn
                    near = (e1 - e2) + (n1_[p] - n1_[p - 1])
                    far = (se - e3) + (n1_[p + 1] - n1_[p - 2])
                    vn = vm + buoy[p, i - 1] * (27.0 * near - far)
                    if step < STEPS:
                        vel[p, i - 1] = vn
                    top = jnp.abs(vn)
                    peak[p, i - 1] = top if first else jnp.maximum(peak[p, i - 1], top)
                    carry[p] = (v0[p], v1, v2, e2, e1, se, sn)
            return tuple(carry)

        start = tuple(
            (vel[p, begin - 1], vel[p, begin], vel[p, begin + 1], zero, zero, zero, zero) for p in range(PLANES)
        )
        lax.fori_loop(0, chunks, sweep, start)

    block = jnp.concatenate([peak[p, OFF : OFF + half_rows].reshape(half_rows * SUB, LANES) for p in range(PLANES)], axis=1)
    back = fold(
        lax.dot_general(pieces(block, 2), deal_own[...], (((1,), (1,)), ((), ())), preferred_element_type=F32)
    )
    for t in range(4):
        flat[t] = back[:, t * LANES : (t + 1) * LANES]
    for t in range(4):
        for a in range(half_rows // SUB):
            at = (t // 2) * half_rows + a * SUB
            for r in range(SUB):
                out_ref[r, at : at + SUB, (t % 2) * LANES : (t % 2 + 1) * LANES] = flat[
                    t, pl.ds(a * SUB * SUB + r, SUB, stride=SUB), :
                ]

    for copy in sent:
        copy.wait_send()


def on_device(gx_n, gy_n, initial_velocity, background_speed, density, east_modes, north_modes, mode_coef):
    reals, rows, cols = initial_velocity.shape
    kx, ky = north_modes.shape[0], east_modes.shape[1]
    y_n = 4 if gy_n == 16 else 2
    x_n = gy_n // y_n
    wide = rows // 2 + 2 * OFF
    natural = rows + 2 * OFF
    slabs = -(-rows // PER)
    lo_len = 1 + (HALO - 1) // PER + 1
    hi_len = slabs - (rows - HALO) // PER + 1
    sends = 4 + 2 + 4 + 2 + 4 + 2 * (gy_n - 1) + gx_n - 1
    vmem = lambda *shape: pltpu.VMEM(shape, F32)
    scratch = [
        vmem(reals, rows, cols),
        vmem(2, rows, cols),
        vmem(ky, rows),
        vmem(kx, cols),
        vmem(3, SUB, LANES),
        vmem(16, cols),
        vmem(gy_n, ky, reals, mode_coef.shape[2]),
        vmem(gy_n * ky * reals, LANES),
        vmem(gy_n, SUB, LANES),
        vmem(LANES, LANES),
        vmem(gx_n, 3, 16, LANES),
        vmem(LANES, 3 * LANES),
        pltpu.VMEM((3, 2 * LANES, WIDE), BF16),
        vmem(2, ky, rows),
        vmem(2, SUB, LANES),
        vmem(2, SUB, LANES),
        vmem(2, natural * SUB, LANES),
        vmem(natural * SUB, LANES),
        vmem(2, 2, OFF, cols),
        vmem(2, slabs + 3, SUB, LANES),
        vmem(2, slabs + 3, SUB, LANES),
        vmem(2, hi_len, SUB, LANES),
        vmem(2, lo_len, SUB, LANES),
        pltpu.VMEM((4 * LANES, WIDE), BF16),
        pltpu.VMEM((2 * LANES, WIDE), BF16),
        vmem(natural * SUB, LANES),
        vmem(3, natural, LANES),
        vmem(3, natural, LANES),
        vmem(wide, WIDE),
        vmem(wide, WIDE),
        vmem(PLANES, wide, SUB, LANES),
        vmem(PLANES, wide, SUB, LANES),
        vmem(PLANES, wide, SUB, LANES),
        vmem(PLANES, wide, SUB, LANES),
        vmem(PLANES, wide, SUB, LANES),
        vmem(PLANES, wide, SUB, LANES),
        vmem(4, rows // 2 * SUB, LANES),
        pltpu.SemaphoreType.DMA((8,)),
        pltpu.SemaphoreType.DMA((sends,)),
        pltpu.SemaphoreType.DMA((16 + 2 * gy_n + gx_n,)),
    ]
    return pl.pallas_call(
        functools.partial(kernel, (gx_n, gy_n, y_n, kx, ky)),
        out_shape=jax.ShapeDtypeStruct(initial_velocity.shape, F32),
        in_specs=[pl.BlockSpec(memory_space=pltpu.HBM)] * 6,
        out_specs=pl.BlockSpec(memory_space=pltpu.VMEM),
        scratch_shapes=scratch,
        compiler_params=pltpu.CompilerParams(
            collective_id=0, has_side_effects=True, vmem_limit_bytes=60 * 1024 * 1024
        ),
    )(
        initial_velocity,
        background_speed,
        density,
        jnp.transpose(east_modes),
        north_modes,
        jnp.transpose(mode_coef, (1, 0, 2)),
    )


def solution(mesh):
    in_specs = (
        P("row", "gx", "gy"),
        P("gx", "gy"),
        P("gx", "gy"),
        P("gx", "gy"),
        P("gx", "gy"),
        P("row", "gy", None),
    )
    out_specs = P("row", "gx", "gy")
    body = functools.partial(on_device, mesh.shape["gx"], mesh.shape["gy"])
    return jax.shard_map(body, mesh=mesh, in_specs=in_specs, out_specs=out_specs, check_vma=False)
```

```python
import functools

import jax
import jax.numpy as jnp
from jax import lax
from jax.experimental import pallas as pl
from jax.experimental.pallas import tpu as pltpu
from jax.sharding import PartitionSpec as P

MESH = pl.DeviceIdType.MESH
F32 = jnp.float32
STEPS = 6
HALO = 3 * STEPS
OFF = 24
LANES = 128
SUB = 8
PER = LANES // HALO
PLANES = 5
HALF = LANES // 2
WIDE = PLANES * LANES
BF16 = jnp.bfloat16
SCALE = 0.55 / 24.0
GAIN = 0.03


def roll(x, shift, axis=1):
    shift %= x.shape[axis]
    return pltpu.roll(x, shift, axis) if shift else x


def lane_index():
    return lax.broadcasted_iota(jnp.int32, (SUB, LANES), 1)


def pieces(x, count):
    parts = []
    for _ in range(count):
        parts.append(x.astype(BF16))
        x = x - parts[-1].astype(F32)
    return jnp.concatenate(parts, axis=0)


def fold(x):
    n = x.shape[0] // 2
    return x[0:n] + x[n:]


N_LO, N_HI, V_LO, V_HI, D_LO, D_HI, B_LO, B_HI, S_LO, S_HI, LL, LH, HL, HH = range(14)


def kernel(
    dims,
    v_hbm,
    bg_hbm,
    d_hbm,
    e_hbm,
    n_hbm,
    c_hbm,
    out_ref,
    v_in,
    db_in,
    n_in,
    pad_e,
    pad_n,
    c_got,
    c_all,
    eg,
    e_all,
    ng,
    n_all,
    n_parts,
    e_got,
    n_edge,
    n_halo,
    nat,
    side,
    db_halo,
    strip,
    strip_halo,
    corner_lo,
    corner_hi,
    deal_own,
    deal_side,
    panel,
    g_nat,
    b_nat,
    g_wide,
    b_wide,
    vel,
    mod,
    buoy,
    s_e,
    s_n,
    peak,
    flat,
    load_sem,
    send_sem,
    recv_sem,
):
    gx_n, gy_n, y_n, kx, ky = dims
    x_n = gy_n // y_n
    gx, gy = lax.axis_index("gx"), lax.axis_index("gy")
    outer, inner = gy // y_n, lax.rem(gy, y_n)
    lane = lane_index()
    rows = v_hbm.shape[1]
    half_rows = rows // 2
    modes = gy_n * ky

    def gxo(o):
        return lax.rem(gx + o + gx_n, gx_n)

    def gyo(o):
        return lax.rem(gy + o + gy_n, gy_n)

    def peer(e, d):
        return lax.rem(outer + e, x_n) * y_n + lax.rem(inner + d, y_n)

    mid_rows = rows - 2 * OFF
    bands = ((0, OFF), (rows - OFF, OFF), (OFF, mid_rows))
    moves = [(n_hbm, n_in), (d_hbm, db_in.at[0]), (bg_hbm, db_in.at[1])]
    moves += [(v_hbm.at[:, pl.ds(a, n)], v_in.at[:, pl.ds(a, n)]) for a, n in bands]
    moves += [(e_hbm, e_got.at[1, 0]), (c_hbm, c_got.at[0])]
    loads = [pltpu.make_async_copy(src, dst, load_sem.at[i]) for i, (src, dst) in enumerate(moves)]
    for load in loads:
        load.start()

    in_x = {-1: gx > 0, 0: None, 1: gx < gx_n - 1}
    in_y = {-1: gy > 0, 0: None, 1: gy < gy_n - 1}

    def inside(a, b):
        conditions = [c for c in (in_x[a], in_y[b]) if c is not None]
        return functools.reduce(jnp.logical_and, conditions) if conditions else None

    def under(condition, act):
        if condition is None:
            act()
        else:
            pl.when(condition)(act)

    partners = [({"gx": gxo(a), "gy": gyo(b)}, inside(a, b)) for a in (-1, 0, 1) for b in (-1, 0, 1) if a or b]
    partners += [({"gx": gxo(a), "gy": peer(0, d)}, in_x[a]) for a in (-1, 0, 1) for d in range(1, y_n)]
    partners += [({"gy": peer(e, 0)}, None) for e in range(1, x_n)]
    partners += [({"gx": gxo(o)}, None) for o in range(1, gx_n)]
    barrier = pltpu.get_barrier_semaphore()
    expected = jnp.int32(0)
    for partner, condition in partners:
        under(
            condition,
            lambda partner=partner: pl.semaphore_signal(barrier, inc=1, device_id=partner, device_id_type=MESH),
        )
        expected += 1 if condition is None else jnp.where(condition, 1, 0)

    sent = []

    def send(src, dst, slot, target, condition=None):
        copy = pltpu.make_async_remote_copy(
            src_ref=src,
            dst_ref=dst,
            send_sem=send_sem.at[len(sent)],
            recv_sem=recv_sem.at[slot],
            device_id=target,
            device_id_type=MESH,
        )
        under(condition, copy.start)
        sent.append((copy, condition))

    def arrived(dst, slot, condition=None):
        under(condition, pltpu.make_async_copy(dst, dst, recv_sem.at[slot]).wait)
        if condition is not None:

            @pl.when(jnp.logical_not(condition))
            def _():
                dst[...] = jnp.zeros(dst.shape, dst.dtype)

    z_base = 14
    c_base = z_base + 3 * y_n
    e_base = c_base + gy_n
    n_base = e_base + gy_n

    pad_e[...] = jnp.zeros_like(pad_e)
    pad_n[...] = jnp.zeros_like(pad_n)
    e_all[...] = jnp.zeros_like(e_all)
    n_all[...] = jnp.zeros_like(n_all)

    pl.semaphore_wait(barrier, expected)

    for d in range(y_n):
        for a in (0, 1, -1) if d else (1, -1):
            slot = z_base + (1 - a) * y_n + d
            send(e_hbm, e_got.at[1 - a, d], slot, {"gx": gxo(a), "gy": peer(0, d)}, in_x[a])
    for d in range(1, y_n):
        send(c_hbm, c_got.at[d], c_base + d, {"gy": peer(0, d)})
    for e in range(1, x_n):
        send(c_hbm, c_got.at[e * y_n], c_base + e * y_n, {"gy": peer(e, 0)})

    for src, lo, hi, q in ((d_hbm, D_LO, D_HI, 0), (bg_hbm, B_LO, B_HI, 1)):
        send(src.at[pl.ds(rows - OFF, OFF)], db_halo.at[0, q], lo, {"gx": gxo(1)}, in_x[1])
        send(src.at[pl.ds(0, OFF)], db_halo.at[1, q], hi, {"gx": gxo(-1)}, in_x[-1])

    loads[0].wait()
    pad_n[0:kx, :] = n_in[...]
    n0, n1 = (pad_n[0:SUB, 0:LANES], pad_n[0:SUB, LANES:]), (pad_n[SUB:, 0:LANES], pad_n[SUB:, LANES:])
    n_edge[0] = jnp.where(lane < HALO, n0[0], roll(n1[0], HALO))
    n_edge[1] = jnp.where(lane < HALO, roll(n0[1], HALO), roll(n1[1], 2 * HALO))
    send(n_edge.at[1], n_halo.at[0], N_LO, {"gy": gyo(1)}, in_y[1])
    send(n_edge.at[0], n_halo.at[1], N_HI, {"gy": gyo(-1)}, in_y[-1])

    def lead(a):
        at = pl.multiple_of(a * SUB, SUB)
        for r in range(SUB):
            for t in range(2):
                nat[t, pl.ds((OFF + a * SUB) * SUB + r, SUB, stride=SUB), :] = v_in[
                    r, pl.ds(at, SUB), t * LANES : (t + 1) * LANES
                ]

    edge = HALO * SUB

    def own(first):
        return nat.at[:, pl.ds((OFF + first) * SUB, edge)]

    for k, (first, count) in enumerate(bands):
        loads[3 + k].wait()
        pl.loop(first // SUB, (first + count) // SUB)(lead)
        if k == 0:
            send(own(0), own(rows), V_HI, {"gx": gxo(-1)}, in_x[-1])
        if k == 1:
            send(own(rows - HALO), own(-HALO), V_LO, {"gx": gxo(1)}, in_x[1])

    loads[1].wait()
    loads[2].wait()

    def tile(t, i):
        return nat[t, pl.ds(pl.multiple_of((OFF + i) * SUB, SUB), SUB), :]

    full = rows // PER

    def pack(g, count):
        low = jnp.zeros((SUB, LANES), F32)
        high = jnp.zeros((SUB, LANES), F32)
        for p in range(count):
            here = (lane >= p * HALO) & (lane < (p + 1) * HALO)
            low = jnp.where(here, roll(tile(0, g * PER + p), p * HALO), low)
            high = jnp.where(here, roll(tile(1, g * PER + p), (p + 1) * HALO), high)
        strip[0, 1 + g] = low
        strip[1, 1 + g] = high

    pl.loop(0, full)(lambda g: pack(g, PER))
    slabs = full
    if rows % PER:
        pack(full, rows % PER)
        slabs += 1
    hi_tile = rows // SUB - 3
    groups = ((0, range(0, 3)), (slabs + 1, range(hi_tile, hi_tile + 3)), (slabs + 2, range(3, hi_tile)))
    for slab, blocks in groups:
        low = jnp.zeros((SUB, LANES), F32)
        high = jnp.zeros((SUB, LANES), F32)
        for j, a in enumerate(blocks):
            for q in range(2):
                p = 2 * j + q
                here = (lane >= p * HALO) & (lane < (p + 1) * HALO)
                low = jnp.where(here, roll(db_in[q, a * SUB : (a + 1) * SUB, 0:LANES], p * HALO), low)
                high = jnp.where(here, roll(db_in[q, a * SUB : (a + 1) * SUB, LANES:], (p + 1) * HALO), high)
        strip[0, slab] = low
        strip[1, slab] = high
    first_hi = (rows - HALO) // PER
    lo_len, hi_len = corner_hi.shape[1], corner_lo.shape[1]
    lo_rows, hi_rows = pl.ds(0, lo_len), pl.ds(1 + first_hi, hi_len)
    send(strip.at[1], strip_halo.at[0], S_LO, {"gy": gyo(1)}, in_y[1])
    send(strip.at[0], strip_halo.at[1], S_HI, {"gy": gyo(-1)}, in_y[-1])
    send(strip.at[1, hi_rows], corner_lo.at[0], LL, {"gx": gxo(1), "gy": gyo(1)}, inside(1, 1))
    send(strip.at[0, hi_rows], corner_lo.at[1], LH, {"gx": gxo(1), "gy": gyo(-1)}, inside(1, -1))
    send(strip.at[1, lo_rows], corner_hi.at[0], HL, {"gx": gxo(-1), "gy": gyo(1)}, inside(-1, 1))
    send(strip.at[0, lo_rows], corner_hi.at[1], HH, {"gx": gxo(-1), "gy": gyo(-1)}, inside(-1, -1))

    loads[6].wait()
    for d in sorted(range(y_n), key=lambda d: min(d, y_n - d)):
        if d:
            arrived(c_got.at[d], c_base + d)
            for e in range(1, x_n):
                send(c_got.at[d], c_got.at[e * y_n + d], c_base + e * y_n + d, {"gy": peer(e, 0)})
        for k in range(3):
            if k != 1 or d:
                arrived(e_got.at[k, d], z_base + k * y_n + d, in_x[k - 1])
            pad_e[k, 0:ky, 0:rows] = e_got[k, d]
        eg[d] = jnp.where(
            lane < OFF,
            roll(pad_e[0], OFF - rows),
            jnp.where(lane < OFF + rows, roll(pad_e[1], OFF), roll(pad_e[2], OFF + rows)),
        )
        for e in range(1, x_n):
            send(eg.at[d], eg.at[e * y_n + d], e_base + e * y_n + d, {"gy": peer(e, 0)})

    arrived(n_halo.at[0], N_LO, in_y[-1])
    arrived(n_halo.at[1], N_HI, in_y[1])

    def flank(west, east):
        return jnp.where(lane < HALO, west, jnp.where(lane < 2 * HALO, east, 0.0))

    for half, (t0, t1) in enumerate((n0, n1)):
        beside = flank(roll(n_halo[0], -half * HALO), roll(n_halo[1], (1 - half) * HALO))
        for t, value in enumerate((t0, t1, beside)):
            ng[gx, t, half * SUB : (half + 1) * SUB, :] = value
    for o in range(1, gx_n):
        send(ng.at[gx], ng.at[gx], n_base + o, {"gx": gxo(o)})

    for half in range(2):
        for p in range(PLANES):
            for ref, n in ((deal_own, 2 * LANES), (deal_side, LANES)):
                k = lax.broadcasted_iota(jnp.int32, (n, LANES), 0)
                l = lax.broadcasted_iota(jnp.int32, (n, LANES), 1) - half * HALF
                if n == LANES:
                    index = jnp.where(k < HALO, k, jnp.where(k < 2 * HALO, k + 2 * LANES, -1))
                else:
                    index = k + HALO
                hit = (PLANES * l + p == index) & (l >= 0) & (l < HALF)
                ref[half * n : (half + 1) * n, p * LANES : (p + 1) * LANES] = jnp.where(hit, 1.0, 0.0).astype(BF16)

    def dealt(natural, firsts, count, apart, middle, beside):
        def tiles(ts, shift):
            return jnp.concatenate(
                [jnp.concatenate([natural(t, pl.ds(f + shift, count)) for t in ts], axis=1) for f in firsts], axis=0
            )

        total = None
        for wanted, ts, deal in ((middle, (0, 1), deal_own), (beside, (2,), deal_side)):
            if wanted:
                left = pieces(jnp.concatenate([tiles(ts, 0), tiles(ts, apart)], axis=1), 2)
                term = jnp.dot(left, deal[...], preferred_element_type=F32)
                total = term if total is None else total + term
        return fold(total)

    def deal_velocity(firsts, count, middle, beside):
        out = dealt(
            lambda t, at: nat[t, at, :] if t < 2 else side[at, :],
            [f * SUB for f in firsts],
            count * SUB,
            half_rows * SUB,
            middle,
            beside,
        )
        for k, f in enumerate(firsts):
            for u in range(count):
                for p in range(PLANES):
                    at = (k * count + u) * SUB
                    value = out[at : at + SUB, p * LANES : (p + 1) * LANES]
                    vel[p, f + u] = value if middle else vel[p, f + u] + value

    wide_rows = vel.shape[1]
    deal_velocity([OFF], half_rows, True, False)

    for slot in range(y_n, gy_n):
        arrived(c_got.at[slot], c_base + slot)
        arrived(eg.at[slot], e_base + slot)
    loads[7].wait()
    c_all[...] = jnp.zeros_like(c_all)
    for slot in range(gy_n):
        e_all[slot * ky : (slot + 1) * ky, :] = eg[slot, 0:ky, :]
        for k in range(ky):
            at = (slot * ky + k) * SUB
            c_all[at : at + SUB, 0 : c_got.shape[3]] = c_got[slot, k]
    nat_rows = OFF + rows + OFF
    lhs = jnp.transpose(e_all[...])[0:nat_rows, 0:modes]
    for r in range(SUB):
        rhs = c_all[pl.ds(r, modes, stride=SUB), :]
        panel[pl.ds(r, nat_rows, stride=SUB), :] = jnp.dot(
            lhs, rhs, precision=lax.Precision.HIGHEST, preferred_element_type=F32
        )

    for o in range(1, gx_n):
        at = gxo(-o)
        arrived(ng.at[at], n_base + o)
    for b in range(gx_n):
        for t in range(3):
            n_all[b * kx : (b + 1) * kx, t * LANES : (t + 1) * LANES] = ng[b, t, 0:kx, :]
    split = pieces(n_all[...], 3)
    lower = jnp.dot(split[:, 0 : 2 * LANES], deal_own[0 : 2 * LANES, :], preferred_element_type=F32)
    lower += jnp.dot(split[:, 2 * LANES :], deal_side[0:LANES, :], preferred_element_type=F32)
    for p in range(PLANES):
        at = slice(p * LANES, (p + 1) * LANES)
        for j in range(3):
            part = lower[j * LANES : (j + 1) * LANES, at]
            n_parts[j, 0:LANES, at] = part.astype(BF16)
            n_parts[j, LANES:, at] = roll(part, HALF).astype(BF16)

    arrived(strip_halo.at[0], S_LO, in_y[-1])
    arrived(strip_halo.at[1], S_HI, in_y[1])
    for s in range(2):
        for q in range(2):
            arrived(db_halo.at[s, q], (D_LO, D_HI, B_LO, B_HI)[2 * q + s], in_x[2 * s - 1])
    for s in range(2):
        arrived(corner_lo.at[s], (LL, LH)[s], inside(-1, 2 * s - 1))
        arrived(corner_hi.at[s], (HL, HH)[s], inside(1, 2 * s - 1))
    tiles = rows // SUB
    for b in range(tiles + 6):
        values = []
        for q in range(2):
            if b < 3:
                body, a = db_halo.at[0, q], b
                w, e = (corner_lo[s, hi_len - 1] for s in range(2))
                p = 2 * b + q
            elif b < tiles + 3:
                body, a = db_in.at[q], b - 3
                slab, blocks = next(g for g in groups if a in g[1])
                w, e = (strip_halo[s, slab] for s in range(2))
                p = 2 * (a - blocks[0]) + q
            else:
                body, a = db_halo.at[1, q], b - 3 - tiles
                w, e = (corner_hi[s, 0] for s in range(2))
                p = 2 * a + q
            t0, t1 = (body[a * SUB : (a + 1) * SUB, t * LANES : (t + 1) * LANES] for t in range(2))
            values.append((t0, t1, flank(roll(w, -p * HALO), roll(e, (1 - p) * HALO))))
        here = slice(b * SUB, (b + 1) * SUB)
        for t in range(3):
            d, s = values[0][t], values[1][t]
            g_nat[t, here, :] = SCALE * d * s * s
            b_nat[t, here, :] = jnp.where(d > 0.0, SCALE / jnp.where(d > 0.0, d, 1.0), 0.0)
    for natural, out in ((g_nat, g_wide), (b_nat, b_wide)):
        out[...] = dealt(lambda t, at, natural=natural: natural[t, at, :], [0], wide_rows, half_rows, True, True)

    begin = OFF - HALO
    chunk = half_rows // 2 + HALO
    for c in range(2):
        n = chunk * SUB
        first = begin + c * chunk
        near, far = (slice((first + a) * SUB, (first + a) * SUB + n) for a in (0, half_rows))
        left = pieces(jnp.concatenate([panel[near, :], panel[far, :]], axis=1), 3)
        a = jnp.dot(left, n_parts[0], preferred_element_type=F32)
        b = jnp.dot(left[0 : 2 * n], n_parts[1], preferred_element_type=F32)
        field = a[0:n] + (
            (a[n : 2 * n] + b[0:n])
            + (a[2 * n :] + b[n:] + jnp.dot(left[0:n], n_parts[2], preferred_element_type=F32))
        )
        for p in range(PLANES):
            at = slice(p * LANES, (p + 1) * LANES)
            g, w = g_wide[first : first + chunk, at], b_wide[first : first + chunk, at]
            for u in range(chunk):
                q = 1.0 + GAIN * jnp.tanh(field[u * SUB : (u + 1) * SUB, at])
                mod[p, first + u] = jnp.broadcast_to(g[u : u + 1], (SUB, LANES)) * (q * q)
                buoy[p, first + u] = jnp.broadcast_to(w[u : u + 1], (SUB, LANES))

    def unpack(west, east, p):
        return flank(roll(west, -p * HALO), roll(east, (1 - p) * HALO))

    def own_sides(g, count):
        for p in range(count):
            at = pl.multiple_of((OFF + g * PER + p) * SUB, SUB)
            side[pl.ds(at, SUB), :] = unpack(strip_halo[0, 1 + g], strip_halo[1, 1 + g], p)

    pl.loop(0, full)(lambda g: own_sides(g, PER))
    if rows % PER:
        own_sides(full, rows % PER)
    deal_velocity([OFF], half_rows, False, True)

    arrived(own(-HALO), V_LO, in_x[-1])
    arrived(own(rows), V_HI, in_x[1])
    for i in range(HALO):
        for corner, row, at, slab in (
            (corner_lo, rows - HALO + i, OFF - HALO + i, (rows - HALO + i) // PER - first_hi),
            (corner_hi, i, OFF + rows + i, 1 + i // PER),
        ):
            side[at * SUB : (at + 1) * SUB, :] = unpack(corner[0, slab], corner[1, slab], row % PER)
    deal_velocity([0, OFF + half_rows], OFF, True, True)

    zero = jnp.zeros((SUB, LANES), F32)
    for step in range(1, STEPS + 1):
        begin = OFF - HALO + 3 * step - 2
        count = half_rows + 2 * HALO + 3 - 6 * step
        unroll = min(range(11, 15), key=lambda n: -count % n)
        chunks = -(-count // unroll)

        def sweep(c, carry, begin=begin, unroll=unroll, first=step == 1):
            carry = list(carry)
            for u in range(unroll):
                i = begin + c * unroll + u
                v0 = [carry[p][1] for p in range(PLANES)]
                n1_ = [carry[p][6] for p in range(PLANES)]
                v0 += [roll(v0[0], -1), roll(v0[1], -1), roll(v0[-1], 1)]
                n1_ += [roll(n1_[0], -1), roll(n1_[-2], 1), roll(n1_[-1], 1)]
                for p in range(PLANES):
                    vm, _, v1, e3, e2, e1, _ = carry[p]
                    v2 = vel[p, i + 2]
                    m = mod[p, i]
                    ge = 27.0 * (v1 - v0[p]) - (v2 - vm)
                    gn = 27.0 * (v0[p + 1] - v0[p]) - (v0[p + 2] - v0[p - 1])
                    se, sn = m * ge, m * gn
                    if not first:
                        se, sn = s_e[p, i] + se, s_n[p, i] + sn
                    if step < STEPS:
                        s_e[p, i] = se
                        s_n[p, i] = sn
                    near = (e1 - e2) + (n1_[p] - n1_[p - 1])
                    far = (se - e3) + (n1_[p + 1] - n1_[p - 2])
                    vn = vm + buoy[p, i - 1] * (27.0 * near - far)
                    if step < STEPS:
                        vel[p, i - 1] = vn
                    top = jnp.abs(vn)
                    peak[p, i - 1] = top if first else jnp.maximum(peak[p, i - 1], top)
                    carry[p] = (v0[p], v1, v2, e2, e1, se, sn)
            return tuple(carry)

        start = tuple(
            (vel[p, begin - 1], vel[p, begin], vel[p, begin + 1], zero, zero, zero, zero) for p in range(PLANES)
        )
        lax.fori_loop(0, chunks, sweep, start)

    block = jnp.concatenate([peak[p, OFF : OFF + half_rows].reshape(half_rows * SUB, LANES) for p in range(PLANES)], axis=1)
    back = fold(
        lax.dot_general(pieces(block, 2), deal_own[...], (((1,), (1,)), ((), ())), preferred_element_type=F32)
    )
    for t in range(4):
        flat[t] = back[:, t * LANES : (t + 1) * LANES]
    for t in range(4):
        for a in range(half_rows // SUB):
            at = (t // 2) * half_rows + a * SUB
            for r in range(SUB):
                out_ref[r, at : at + SUB, (t % 2) * LANES : (t % 2 + 1) * LANES] = flat[
                    t, pl.ds(a * SUB * SUB + r, SUB, stride=SUB), :
                ]

    for copy, condition in sent:
        under(condition, copy.wait_send)


def on_device(gx_n, gy_n, initial_velocity, background_speed, density, east_modes, north_modes, mode_coef):
    reals, rows, cols = initial_velocity.shape
    kx, ky = north_modes.shape[0], east_modes.shape[1]
    y_n = 4 if gy_n == 16 else 2
    x_n = gy_n // y_n
    wide = rows // 2 + 2 * OFF
    natural = rows + 2 * OFF
    slabs = -(-rows // PER)
    lo_len = 1 + (HALO - 1) // PER + 1
    hi_len = slabs - (rows - HALO) // PER + 1
    sends = 14 + (3 * y_n - 1) + (gy_n - 1) + (x_n - 1) * y_n + gx_n - 1
    vmem = lambda *shape: pltpu.VMEM(shape, F32)
    scratch = [
        vmem(reals, rows, cols),
        vmem(2, rows, cols),
        vmem(kx, cols),
        vmem(3, SUB, LANES),
        vmem(16, cols),
        vmem(gy_n, ky, reals, mode_coef.shape[2]),
        vmem(gy_n * ky * reals, LANES),
        vmem(gy_n, SUB, LANES),
        vmem(LANES, LANES),
        vmem(gx_n, 3, 16, LANES),
        vmem(LANES, 3 * LANES),
        pltpu.VMEM((3, 2 * LANES, WIDE), BF16),
        vmem(3, y_n, ky, rows),
        vmem(2, SUB, LANES),
        vmem(2, SUB, LANES),
        vmem(2, natural * SUB, LANES),
        vmem(natural * SUB, LANES),
        vmem(2, 2, OFF, cols),
        vmem(2, slabs + 3, SUB, LANES),
        vmem(2, slabs + 3, SUB, LANES),
        vmem(2, hi_len, SUB, LANES),
        vmem(2, lo_len, SUB, LANES),
        pltpu.VMEM((4 * LANES, WIDE), BF16),
        pltpu.VMEM((2 * LANES, WIDE), BF16),
        vmem(natural * SUB, LANES),
        vmem(3, natural, LANES),
        vmem(3, natural, LANES),
        vmem(wide, WIDE),
        vmem(wide, WIDE),
        vmem(PLANES, wide, SUB, LANES),
        vmem(PLANES, wide, SUB, LANES),
        vmem(PLANES, wide, SUB, LANES),
        vmem(PLANES, wide, SUB, LANES),
        vmem(PLANES, wide, SUB, LANES),
        vmem(PLANES, wide, SUB, LANES),
        vmem(4, rows // 2 * SUB, LANES),
        pltpu.SemaphoreType.DMA((8,)),
        pltpu.SemaphoreType.DMA((sends,)),
        pltpu.SemaphoreType.DMA((14 + 3 * y_n + 2 * gy_n + gx_n,)),
    ]
    return pl.pallas_call(
        functools.partial(kernel, (gx_n, gy_n, y_n, kx, ky)),
        out_shape=jax.ShapeDtypeStruct(initial_velocity.shape, F32),
        in_specs=[pl.BlockSpec(memory_space=pltpu.HBM)] * 6,
        out_specs=pl.BlockSpec(memory_space=pltpu.VMEM),
        scratch_shapes=scratch,
        compiler_params=pltpu.CompilerParams(
            collective_id=0, has_side_effects=True, vmem_limit_bytes=60 * 1024 * 1024
        ),
    )(
        initial_velocity,
        background_speed,
        density,
        jnp.transpose(east_modes),
        north_modes,
        jnp.transpose(mode_coef, (1, 0, 2)),
    )


def solution(mesh):
    in_specs = (
        P("row", "gx", "gy"),
        P("gx", "gy"),
        P("gx", "gy"),
        P("gx", "gy"),
        P("gx", "gy"),
        P("row", "gy", None),
    )
    out_specs = P("row", "gx", "gy")
    body = functools.partial(on_device, mesh.shape["gx"], mesh.shape["gy"])
    return jax.shard_map(body, mesh=mesh, in_specs=in_specs, out_specs=out_specs, check_vma=False)
```
